512 devices in a mesh: harm: 8 (over x, z_hi), row: 64 (over z_lo, y, core).
Axes of the slice: x: 4, y: 4, z: 16 (z_hi: 2, z_lo: 8; z = z_hi * 8 + z_lo), core: 2. Of those that a mesh axis runs over, the one named last changes fastest.
Arguments:
- currents: float32 [8, 4, 2, 512, 512], P('harm', None, None, 'row'), may hold values from -6 to 6
- incident: float32 [8, 4, 2, 512, 512], P('harm', None, None, 'row'), may hold values from -6 to 6
- kernel: float32 [8, 4, 4, 2, 1024, 1024], P('harm', None, None, None, 'row'), may hold values from -4 to 4
- port_weights: float32 [4], replicated, may hold values from 0.2 to 0.6
- bias_level: int32 [512, 512], P('row', 'harm'), may hold values from 0 to 15
Outputs:
- residual: float32 [8, 4, 2, 512, 512], P('harm', None, None, 'row')
The draws below stay inside these ranges and needn't reach their ends.
Inputs may be any that keep to these rules, and one draw needn't show every extreme that they name: `bias_level`: integer capacitance level of each cell's varactor.
All inputs are finite; a program needn't handle non-finite values.
Results may differ from the reference program's by a relative error of at most 0.0003.
Values sent between devices are 32-bit elements; how exact they have to be, the bound alone decides.
A program may use at most 64 MiB of HBM per device.

```python
import jax
import jax.numpy as jnp
from jax import lax

HARMS = 8
BASIS = 4
ROWS = 512
COLS = 512
SAMPLES = 32
PAD_R = 1024
PAD_C = 1024


def set_ends(array, rng, low, top_value):
    spot = [jax.random.randint(jax.random.fold_in(rng, axis), (), 0, length) for axis, length in enumerate(array.shape)]
    longest = array.shape.index(max(array.shape))
    neighbour = spot[:longest] + [(spot[longest] + 1) % array.shape[longest]] + spot[longest + 1:]
    return array.at[tuple(spot)].set(low).at[tuple(neighbour)].set(top_value)


def level_of(rng, dims, cuts, low, largest):
    gain, own = 1.0, jax.random.fold_in(rng, 6)
    for axis_at, shards_of in cuts:
        heights = jnp.exp(jax.random.uniform(jax.random.fold_in(own, axis_at), (shards_of,), jnp.float32, low / len(cuts), largest / len(cuts)))
        gain = gain * jnp.repeat(heights, dims[axis_at] // shards_of).reshape([-1 if axis == axis_at else 1 for axis in range(len(dims))])
    return gain


def scatter_about(own_key, extent, deviation, most, pieces=(), held_as=jnp.bfloat16):
    factor_of = level_of(own_key, extent, pieces, -0.22, 0.18) if pieces else 1.0
    entries = jax.random.normal(own_key, extent, jnp.float32) * deviation * factor_of
    return jnp.minimum(jnp.maximum(entries, -most), most).astype(held_as)


def setup_inputs(seed: int = 0) -> dict:
    key_of = jax.random.split(jax.random.key(seed), 6)
    return {
        "currents": scatter_about(key_of[0], (HARMS, BASIS, 2, ROWS, COLS), 1.0, 6.0, ((0, 8), (3, 64)), jnp.float32),
        "incident": scatter_about(key_of[1], (HARMS, BASIS, 2, ROWS, COLS), 1.0, 6.0, ((0, 8), (3, 64)), jnp.float32),
        "kernel": scatter_about(key_of[2], (HARMS, BASIS, BASIS, 2, PAD_C, PAD_R), 0.5, 4.0, ((0, 8), (4, 64)), jnp.float32),
        "port_weights": jnp.clip(jax.random.uniform(key_of[3], (BASIS,), jnp.float32, 0.2, 0.6), 0.2, 0.6),
        "bias_level": set_ends(jax.random.randint(key_of[4], (ROWS, COLS), 0, 16), jax.random.fold_in(key_of[4], 1), 0, 15).astype(jnp.int32),
    }


def harmonic_table(count, samples):
    numbers = jnp.arange(1, count + 1, dtype=jnp.int32)[:, None] * jnp.arange(samples, dtype=jnp.int32)[None, :]
    angle = (2.0 * jnp.pi / samples) * (numbers % samples).astype(jnp.float32)
    return jnp.stack([jnp.cos(angle), -jnp.sin(angle)], axis=1)


def one_field(pair):
    current, green = pair
    source = lax.complex(current[:, 0], current[:, 1])
    spectrum = jnp.fft.fft2(source, s=(PAD_R, PAD_C))
    green_c = lax.complex(green[:, :, 0], green[:, :, 1])
    green_c = jnp.swapaxes(green_c, -1, -2)
    mixed = jnp.sum(green_c * spectrum[None], axis=1)
    back = jnp.fft.ifft2(mixed)[:, :ROWS, :COLS]
    return jnp.stack([jnp.real(back), jnp.imag(back)], axis=1).astype(currents_type(current))


def currents_type(current):
    return current.dtype


def reference(currents, incident, kernel, port_weights, bias_level):
    field = lax.map(one_field, (currents, kernel))
    total = field + incident
    volt = jnp.sum(port_weights[None, :, None, None, None] * total, axis=1)
    table = harmonic_table(HARMS, SAMPLES)
    wave = jnp.einsum('hprc,hpn->nrc', volt, table, precision=lax.Precision.HIGHEST)
    cap = 0.05 + 0.02 * bias_level.astype(jnp.float32)
    conduct = 0.05 * (jnp.exp(wave / 4.0) - 1.0)
    charge = cap[None] * (wave + 0.2 * wave * wave)
    conduct_h = jnp.einsum('nrc,hpn->hprc', conduct, table, precision=lax.Precision.HIGHEST) * (2.0 / SAMPLES)
    charge_h = jnp.einsum('nrc,hpn->hprc', charge, table, precision=lax.Precision.HIGHEST) * (2.0 / SAMPLES)
    order = (0.25 * jnp.arange(1, HARMS + 1, dtype=jnp.int32).astype(jnp.float32))[:, None, None]
    diode = jnp.stack([conduct_h[:, 0] - order * charge_h[:, 1], conduct_h[:, 1] + order * charge_h[:, 0]], axis=1)
    return total - port_weights[None, :, None, None, None] * diode[:, None]
```

```python
import functools
import math

import jax
import jax.numpy as jnp
import ml_dtypes
import numpy as np
from jax import lax
from jax.experimental import pallas as pl
from jax.experimental.pallas import tpu as pltpu
from jax.sharding import PartitionSpec as P

MESH = pl.DeviceIdType.MESH
F32 = jnp.float32
BF16 = jnp.bfloat16
HARMS = 8
SAMPLES = 32
NROW = 64
PAD = 1024


def split_np(table):
    high = table.astype(ml_dtypes.bfloat16)
    low = (table - high.astype(np.float64)).astype(ml_dtypes.bfloat16)
    return high, low


def cos_sin(product, length):
    angle = 2.0 * np.pi / length * (product % length).astype(np.float64)
    return np.cos(angle), np.sin(angle)


@functools.lru_cache(maxsize=None)
def tables():
    c, s = cos_sin(np.arange(512)[:, None] * np.arange(PAD)[None, :], PAD)
    w = np.concatenate([c.reshape(512, 4, 256), s.reshape(512, 4, 256)], axis=2).transpose(1, 0, 2)
    w1 = np.stack(split_np(w))
    r = 8 * np.arange(64)[None, :, None] + np.arange(8)[:, None, None]
    c, s = cos_sin(r * np.arange(128)[None, None, :], PAD)
    hi, lo = split_np(np.concatenate([c, s], axis=2))
    e2 = np.concatenate([hi, hi, lo], axis=1)
    c, s = cos_sin(r * np.arange(128)[None, None, :], PAD)
    hi, lo = split_np(np.concatenate([c, s], axis=1) / float(PAD * PAD))
    e3 = np.concatenate([hi, hi, lo], axis=2)
    c, s = cos_sin(np.arange(PAD)[:, None] * np.arange(512)[None, :], PAD)
    w = np.concatenate([c.reshape(PAD, 4, 128), s.reshape(PAD, 4, 128)], axis=2).transpose(1, 0, 2)
    w4 = np.stack(split_np(w))
    k = np.stack([2 * np.arange(4) + 2, 2 * np.arange(4) + 1], axis=1)
    c, s = cos_sin(k[:, None, :] * np.arange(16)[None, :, None], SAMPLES)
    co = np.stack([c, s]) * (2.0 / SAMPLES)
    coef = np.repeat(co, 64, axis=3).astype(np.float32).reshape(128, 128)
    return w1, e2, e3, w4, coef


def dft8(z, sign):
    def add(a, b):
        return (a[0] + b[0], a[1] + b[1])

    def sub(a, b):
        return (a[0] - b[0], a[1] - b[1])

    def turn(a):
        return (-a[1], a[0]) if sign > 0 else (a[1], -a[0])

    def four(a0, a1, a2, a3):
        p, m = add(a0, a2), sub(a0, a2)
        q, d = add(a1, a3), turn(sub(a1, a3))
        return [add(p, q), add(m, d), sub(p, q), sub(m, d)]

    even = four(z[0], z[2], z[4], z[6])
    odd = four(z[1], z[3], z[5], z[7])
    h = math.sqrt(0.5)
    o1, o3 = turn(odd[1]), turn(odd[3])
    odd = [
        odd[0],
        ((odd[1][0] + o1[0]) * h, (odd[1][1] + o1[1]) * h),
        turn(odd[2]),
        ((o3[0] - odd[3][0]) * h, (o3[1] - odd[3][1]) * h),
    ]
    return [add(e, o) for e, o in zip(even, odd)] + [sub(e, o) for e, o in zip(even, odd)]


def split(x):
    high = x.astype(BF16)
    return high, (x - high.astype(F32)).astype(BF16)


def lanes_of(shape):
    return lax.broadcasted_iota(jnp.int32, shape, 1)


def swap_blocks(v):
    v = list(v)
    block = lanes_of(v[0].shape) // 16
    for s in (4, 2, 1):
        keep = (block & s) == 0
        for a in range(8):
            if a & s:
                continue
            x, y = v[a], v[a + s]
            v[a] = jnp.where(keep, x, pltpu.roll(y, 16 * s, 1))
            v[a + s] = jnp.where(keep, pltpu.roll(x, 128 - 16 * s, 1), y)
    return v


def halves(x, y):
    left = lanes_of(x.shape) < 64
    return (
        jnp.where(left, x, pltpu.roll(y, 64, 1)),
        jnp.where(left, pltpu.roll(x, 64, 1), y),
    )


def dot(a, b, ca=1, cb=0):
    return lax.dot_general(a, b, (((ca,), (cb,)), ((), ())), preferred_element_type=F32)


def tile(ref, i):
    return ref.at[pl.ds(pl.multiple_of(8 * i, 8), 8), :]


def spread(axis, count, src, dst, send, recv):
    me = lax.axis_index(axis)

    def step(i, carry):
        to = lax.rem(me + i, count)
        pltpu.make_async_remote_copy(
            src_ref=tile(src, to),
            dst_ref=tile(dst, me),
            send_sem=send,
            recv_sem=recv,
            device_id={axis: to},
            device_id_type=MESH,
        ).start()
        return carry

    lax.fori_loop(1, count, step, 0)
    tile(dst, me)[...] = tile(src, me)[...]


def settle(count, src, dst, send, recv):
    rows = pl.ds(0, 8 * (count - 1))
    pltpu.make_async_copy(dst.at[rows], dst.at[rows], recv).wait()
    pltpu.make_async_copy(src.at[rows], src.at[rows], send).wait()


def kernel(
    cur, inc, bias, coef, pw, g_hbm, w1_hbm, e2_hbm, e3_hbm, w4_hbm, out,
    g, w1, e2, e3, w4, tx1, rx1, zb, yb, tx2, rx2, xk, tot, hs, hr, ds, dr, load, send, recv,
):
    row, harm = lax.axis_index("row"), lax.axis_index("harm")
    loads = [
        pltpu.make_async_copy(a, b, load.at[i])
        for i, (a, b) in enumerate(((w1_hbm, w1), (e2_hbm, e2), (g_hbm, g), (e3_hbm, e3), (w4_hbm, w4)))
    ]
    for c in loads:
        c.start()
    barrier = pltpu.get_barrier_semaphore()

    def greet(axis, me, count):
        def step(i, carry):
            pl.semaphore_signal(
                barrier, inc=1, device_id={axis: lax.rem(me + i, count)}, device_id_type=MESH
            )
            return carry

        lax.fori_loop(1, count, step, 0)

    greet("harm", harm, HARMS)
    greet("row", row, NROW)

    loads[0].wait()
    hi, lo = split(cur[...].reshape(64, 512))
    both = jnp.concatenate([hi, lo], axis=0)
    for j in range(4):
        r1 = dot(both, w1[0, j])
        r = r1[:64] + r1[64:] + dot(hi, w1[1, j])
        r = r.reshape(4, 2, 8, 512)
        for half in range(2):
            c, s = r[..., 128 * half : 128 * half + 128], r[..., 256 + 128 * half : 384 + 128 * half]
            v = [c[b, 0] + s[b, 1] for b in range(4)] + [c[b, 1] - s[b, 0] for b in range(4)]
            for i, x in enumerate(swap_blocks(v)):
                d = 16 * j + 8 * half + i
                tx1[8 * d : 8 * d + 8, :] = x

    pl.semaphore_wait(barrier, HARMS + NROW - 2)
    spread("row", NROW, tx1, rx1, send.at[0], recv.at[0])
    loads[1].wait()
    loads[2].wait()
    settle(NROW, tx1, rx1, send.at[0], recv.at[0])

    def rows_forward(t, carry):
        hi, lo = split(rx1[pl.ds(t, 64, stride=8), :])
        r = dot(jnp.concatenate([hi, lo, hi], axis=0), e2[t], 0, 0)
        p, q = r[:, :128], r[:, 128:]
        zb[t, 0] = p[:64] + q[64:]
        zb[t, 1] = p[64:] - q[:64]
        return carry

    lax.fori_loop(0, 8, rows_forward, 0)

    def combine(i, carry):
        at = pl.ds(pl.multiple_of(8 * i, 8), 8)
        z = dft8([(zb[t, 0, at, :], zb[t, 1, at, :]) for t in range(8)], -1)
        for q in range(8):
            zb[q, 0, at, :], zb[q, 1, at, :] = z[q]
        return carry

    lax.fori_loop(0, 8, combine, 0)

    def mix(i, carry):
        b, kh = i // 2, i % 2
        at = pl.ds(pl.multiple_of(8 * kh, 8), 8)
        f = []
        for q in range(8):
            re = im = None
            for c in range(4):
                src = pl.ds(pl.multiple_of(16 * c + 8 * kh, 8), 8)
                sr, si = zb[q, 0, src, :], zb[q, 1, src, :]
                gr = g[b, c, 0, at, 128 * q : 128 * q + 128]
                gi = g[b, c, 1, at, 128 * q : 128 * q + 128]
                x, y = gr * sr - gi * si, gr * si + gi * sr
                re, im = (x, y) if c == 0 else (re + x, im + y)
            f.append((re, im))
        y = dft8(f, 1)
        for t in range(8):
            yb[t, pl.ds(pl.multiple_of(8 * i, 8), 8), :] = y[t][0]
            yb[t, pl.ds(pl.multiple_of(64 + 8 * i, 8), 8), :] = y[t][1]
        return carry

    lax.fori_loop(0, 8, mix, 0)
    loads[3].wait()

    def rows_inverse(t, carry):
        hi, lo = split(yb[t])
        r = dot(e3[t], jnp.concatenate([hi, lo, hi], axis=1), 1, 1)
        turned = pltpu.roll(r[64:], 64, 1)
        left = lanes_of(turned.shape) < 64
        tx2[pl.ds(t, 64, stride=8), :] = r[:64] + jnp.where(left, -turned, turned)
        return carry

    lax.fori_loop(0, 8, rows_inverse, 0)
    spread("row", NROW, tx2, rx2, send.at[1], recv.at[1])
    loads[4].wait()
    settle(NROW, tx2, rx2, send.at[1], recv.at[1])

    for j in range(8):
        v = swap_blocks([rx2[64 * j + 8 * i : 64 * j + 8 * i + 8, :] for i in range(8)])
        for i in range(8):
            xk[8 * i : 8 * i + 8, 128 * j : 128 * j + 128] = v[i]
    hi, lo = split(xk[...])
    both = jnp.concatenate([hi, lo], axis=0)
    for u in range(4):
        r1 = dot(both, w4[0, u])
        r = r1[:64] + r1[64:] + dot(hi, w4[1, u])
        fields = (r[:32, :128] - r[32:, 128:], r[32:, :128] + r[:32, 128:])
        at = slice(128 * u, 128 * u + 128)
        volt = []
        for p in range(2):
            acc = None
            for b in range(4):
                x = fields[p][8 * b : 8 * b + 8] + inc[b, p, :, at]
                tot[b, p, :, at] = x
                acc = pw[b] * x if b == 0 else acc + pw[b] * x
            volt.append(acc)
        hs[16 * u : 16 * u + 8, :], hs[16 * u + 8 : 16 * u + 16, :] = halves(*volt)

    spread("harm", HARMS, hs, hr, send.at[2], recv.at[2])
    settle(HARMS, hs, hr, send.at[2], recv.at[2])

    left = lanes_of((8, 128)) < 64
    sign = jnp.where(left, 1.0, -1.0)
    volts = []
    for h in range(HARMS):
        v = hr[8 * h : 8 * h + 8, :]
        w = pltpu.roll(v, 64, 1)
        v0, v1 = jnp.where(left, v, w), jnp.where(left, w, v)
        if h % 2 == 0:
            v0, v1 = v0 * sign, v1 * sign
        volts.append((v0, v1))
    level = bias[...].astype(F32)
    cap = 0.05 + 0.02 * jnp.concatenate([level, level], axis=1)
    sums = [[None] * 4 for _ in range(4)]
    for n in range(16):
        wave = None
        for h in range(HARMS):
            angle = 2.0 * math.pi * (((h + 1) * n) % SAMPLES) / SAMPLES
            x = volts[h][0] * math.cos(angle) - volts[h][1] * math.sin(angle)
            wave = x if wave is None else wave + x
        conduct = 0.05 * (jnp.exp(wave * 0.25) - 1.0)
        charge = cap * (wave + 0.2 * wave * wave)
        conduct = conduct * sign + pltpu.roll(conduct, 64, 1)
        charge = charge * sign + pltpu.roll(charge, 64, 1)
        for j in range(4):
            cs = coef[16 * j + n : 16 * j + n + 1, :]
            sn = coef[64 + 16 * j + n : 64 + 16 * j + n + 1, :]
            terms = (conduct * cs, conduct * sn, charge * cs, charge * sn)
            sums[j] = [t if a is None else a + t for a, t in zip(sums[j], terms)]
    for j in range(4):
        order = jnp.where(left, 0.25 * (2 * j + 2), 0.25 * (2 * j + 1))
        cc, cn, qc, qn = sums[j]
        even, odd = halves(cc + order * qn, order * qc - cn)
        ds[16 * j : 16 * j + 8, :] = odd
        ds[16 * j + 8 : 16 * j + 16, :] = even

    spread("harm", HARMS, ds, dr, send.at[3], recv.at[3])
    settle(HARMS, ds, dr, send.at[3], recv.at[3])
    for u in range(4):
        diode = halves(dr[16 * u : 16 * u + 8, :], dr[16 * u + 8 : 16 * u + 16, :])
        at = slice(128 * u, 128 * u + 128)
        for b in range(4):
            for p in range(2):
                out[b, p, :, at] = tot[b, p, :, at] - pw[b] * diode[p]


def body(currents, incident, green, port_weights, bias_level):
    w1, e2, e3, w4, coef = (jnp.asarray(t) for t in tables())
    vmem = pl.BlockSpec(memory_space=pltpu.VMEM)
    smem = pl.BlockSpec(memory_space=pltpu.SMEM)
    anyw = pl.BlockSpec(memory_space=pl.ANY)
    out = pl.pallas_call(
        kernel,
        out_shape=jax.ShapeDtypeStruct((4, 2, 8, 512), F32),
        in_specs=[vmem, vmem, vmem, vmem, smem] + [anyw] * 5,
        out_specs=vmem,
        scratch_shapes=[
            pltpu.VMEM((4, 4, 2, 16, 1024), F32),
            pltpu.VMEM(w1.shape, BF16),
            pltpu.VMEM(e2.shape, BF16),
            pltpu.VMEM(e3.shape, BF16),
            pltpu.VMEM(w4.shape, BF16),
            pltpu.VMEM((512, 128), F32),
            pltpu.VMEM((512, 128), F32),
            pltpu.VMEM((8, 2, 64, 128), F32),
            pltpu.VMEM((8, 128, 128), F32),
            pltpu.VMEM((512, 128), F32),
            pltpu.VMEM((512, 128), F32),
            pltpu.VMEM((64, 1024), F32),
            pltpu.VMEM((4, 2, 8, 512), F32),
            pltpu.VMEM((64, 128), F32),
            pltpu.VMEM((64, 128), F32),
            pltpu.VMEM((64, 128), F32),
            pltpu.VMEM((64, 128), F32),
            pltpu.SemaphoreType.DMA((5,)),
            pltpu.SemaphoreType.DMA((4,)),
            pltpu.SemaphoreType.DMA((4,)),
        ],
        compiler_params=pltpu.CompilerParams(
            collective_id=0, has_side_effects=True, vmem_limit_bytes=48 * 2**20
        ),
        cost_estimate=pl.CostEstimate(flops=5 * 10**9, bytes_accessed=13 * 10**6, transcendentals=16384),
    )(currents[0], incident[0], bias_level, coef, port_weights, green[0], w1, e2, e3, w4)
    return out[None]


def solution(mesh):
    placed = (
        P("harm", None, None, "row", None),
        P("harm", None, None, "row", None),
        P("harm", None, None, None, "row", None),
        P(),
        P("row", "harm"),
    )
    return jax.shard_map(
        body,
        mesh=mesh,
        in_specs=placed,
        out_specs=P("harm", None, None, "row", None),
        check_vma=False,
    )
```

```python
import functools
import math

import jax
import jax.numpy as jnp
import ml_dtypes
import numpy as np
from jax import lax
from jax.experimental import pallas as pl
from jax.experimental.pallas import tpu as pltpu
from jax.sharding import PartitionSpec as P

MESH = pl.DeviceIdType.MESH
F32 = jnp.float32
BF16 = jnp.bfloat16
HARMS = 8
SAMPLES = 32
NROW = 64
PAD = 1024


def split_np(table):
    high = table.astype(ml_dtypes.bfloat16)
    low = (table - high.astype(np.float64)).astype(ml_dtypes.bfloat16)
    return high, low


def cos_sin(product, length):
    angle = 2.0 * np.pi / length * (product % length).astype(np.float64)
    return np.cos(angle), np.sin(angle)


@functools.lru_cache(maxsize=None)
def tables():
    c, s = cos_sin(np.arange(512)[:, None] * np.arange(PAD)[None, :], PAD)
    w = np.concatenate([c.reshape(512, 4, 256), s.reshape(512, 4, 256)], axis=2).transpose(1, 0, 2)
    w1 = np.stack(split_np(w), axis=1)
    r = 8 * np.arange(64)[None, :, None] + np.arange(8)[:, None, None]
    c, s = cos_sin(r * np.arange(128)[None, None, :], PAD)
    hi, lo = split_np(np.concatenate([c, s], axis=2))
    e2 = np.concatenate([hi, hi, lo], axis=1)
    c, s = cos_sin(r * np.arange(128)[None, None, :], PAD)
    hi, lo = split_np(np.concatenate([c, s], axis=1) / float(PAD * PAD))
    e3 = np.concatenate([hi, hi, lo], axis=2)
    c, s = cos_sin(np.arange(PAD)[:, None] * np.arange(512)[None, :], PAD)
    w = np.concatenate([c.reshape(PAD, 4, 128), s.reshape(PAD, 4, 128)], axis=2).transpose(1, 0, 2)
    w4 = np.stack(split_np(w), axis=1)
    return w1, e2, e3, w4


def dft8(z, sign):
    def add(a, b):
        return (a[0] + b[0], a[1] + b[1])

    def sub(a, b):
        return (a[0] - b[0], a[1] - b[1])

    def turn(a):
        return (-a[1], a[0]) if sign > 0 else (a[1], -a[0])

    def four(a0, a1, a2, a3):
        p, m = add(a0, a2), sub(a0, a2)
        q, d = add(a1, a3), turn(sub(a1, a3))
        return [add(p, q), add(m, d), sub(p, q), sub(m, d)]

    even = four(z[0], z[2], z[4], z[6])
    odd = four(z[1], z[3], z[5], z[7])
    h = math.sqrt(0.5)
    o1, o3 = turn(odd[1]), turn(odd[3])
    odd = [
        odd[0],
        ((odd[1][0] + o1[0]) * h, (odd[1][1] + o1[1]) * h),
        turn(odd[2]),
        ((o3[0] - odd[3][0]) * h, (o3[1] - odd[3][1]) * h),
    ]
    return [add(e, o) for e, o in zip(even, odd)] + [sub(e, o) for e, o in zip(even, odd)]


def split(x):
    high = x.astype(BF16)
    return high, (x - high.astype(F32)).astype(BF16)


def lanes_of(shape):
    return lax.broadcasted_iota(jnp.int32, shape, 1)


def swap_blocks(v):
    v = list(v)
    block = lanes_of(v[0].shape) // 16
    for s in (4, 2, 1):
        keep = (block & s) == 0
        for a in range(8):
            if a & s:
                continue
            x, y = v[a], v[a + s]
            v[a] = jnp.where(keep, x, pltpu.roll(y, 16 * s, 1))
            v[a + s] = jnp.where(keep, pltpu.roll(x, 128 - 16 * s, 1), y)
    return v


def dot(a, b, ca=1, cb=0):
    return lax.dot_general(a, b, (((ca,), (cb,)), ((), ())), preferred_element_type=F32)


def tile(ref, i):
    return ref.at[pl.ds(pl.multiple_of(8 * i, 8), 8), :]


def spread(axis, count, src, dst, send, recv):
    me = lax.axis_index(axis)

    def step(i, carry):
        to = lax.rem(me + i, count)
        pltpu.make_async_remote_copy(
            src_ref=tile(src, to),
            dst_ref=tile(dst, me),
            send_sem=send,
            recv_sem=recv,
            device_id={axis: to},
            device_id_type=MESH,
        ).start()
        return carry

    lax.fori_loop(1, count, step, 0)
    tile(dst, me)[...] = tile(src, me)[...]


def settle(count, src, dst, send, recv):
    rows = pl.ds(0, 8 * (count - 1))
    pltpu.make_async_copy(dst.at[rows], dst.at[rows], recv).wait()
    pltpu.make_async_copy(src.at[rows], src.at[rows], send).wait()


def greet(axis, count):
    me = lax.axis_index(axis)

    def step(i, carry):
        pl.semaphore_signal(
            pltpu.get_barrier_semaphore(),
            inc=1,
            device_id={axis: lax.rem(me + i, count)},
            device_id_type=MESH,
        )
        return carry

    lax.fori_loop(1, count, step, 0)


def await_all(count):
    pl.semaphore_wait(pltpu.get_barrier_semaphore(), count)


def rows16(ref, i):
    return ref.at[pl.ds(pl.multiple_of(16 * i, 16), 16), :]


def pass_on(src, dst, to, harm, send, recv):
    @pl.when(to != harm)
    def _():
        pltpu.make_async_remote_copy(
            src_ref=src,
            dst_ref=dst,
            send_sem=send,
            recv_sem=recv,
            device_id={"harm": to},
            device_id_type=MESH,
        ).start()

    @pl.when(to == harm)
    def _():
        dst[...] = src[...]


def finish(count, src, dst, send, recv):
    rows = pl.ds(0, count)
    pltpu.make_async_copy(dst.at[rows], dst.at[rows], recv).wait()
    pltpu.make_async_copy(src.at[rows], src.at[rows], send).wait()


def trig(k, n):
    angle = 2.0 * math.pi * ((k * n) % SAMPLES) / SAMPLES
    return math.cos(angle), math.sin(angle)


def waves(volts):
    out = [None] * SAMPLES
    for n in range(9):
        sums = [None] * 4
        for h in range(HARMS):
            c, s = trig(h + 1, n)
            for i, x in (((h + 1) % 2, volts[h][0] * c), (2 + (h + 1) % 2, volts[h][1] * s)):
                sums[i] = x if sums[i] is None else sums[i] + x
        ce, co, se, so = sums
        p, m, u, v = ce + co, ce - co, se + so, se - so
        out[n] = p - u
        out[16 + n] = m - v
        if n:
            out[16 - n] = m + v
            out[SAMPLES - n] = p + u
    return out


def harmonics(x, numbers):
    sums = [[None, None] for _ in numbers]
    odd = numbers[0] % 2
    for n in range(9):
        if n in (0, 8):
            a, d = x[n], x[16 + n]
            even, flat = (a - d, a - d) if odd else (a + d, a + d)
        else:
            a, b, c, d = x[n], x[SAMPLES - n], x[16 - n], x[16 + n]
            even = (a + b) - (c + d) if odd else (a + b) + (c + d)
            flat = (a - b) + (c - d) if odd else (a - b) - (c - d)
        for i, k in enumerate(numbers):
            for part, (y, w) in enumerate(zip((even, flat), trig(k, n))):
                if abs(w) < 1e-12:
                    continue
                y = y * (w * 2.0 / SAMPLES)
                sums[i][part] = y if sums[i][part] is None else sums[i][part] + y
    return sums


def kernel(
    cur_hbm, inc_hbm, bias_hbm, pw_hbm, g_hbm, w1_hbm, e2_hbm, e3_hbm, w4_hbm, out,
    cur, inc, bias, pw, g, w1, e2, e3, w4, tx1, rx1, zb, yb, tx2, rx2, xk, tot,
    level, hs, hr, ds, dr, load, send, recv,
):
    harm = lax.axis_index("harm")
    x, zhi = harm // 2, lax.rem(harm, 2)
    greet("harm", HARMS)
    greet("row", NROW)
    pairs = [(cur_hbm, cur)] + [(w1_hbm.at[j], w1.at[j]) for j in range(4)]
    pairs += [(bias_hbm, bias), (pw_hbm, pw), (inc_hbm, inc), (e2_hbm, e2), (g_hbm, g), (e3_hbm, e3), (w4_hbm, w4)]
    loads = [pltpu.make_async_copy(a, b, load.at[i]) for i, (a, b) in enumerate(pairs)]
    for c in loads:
        c.start()

    loads[0].wait()
    hi, lo = split(cur[...].reshape(64, 512))
    both = jnp.concatenate([hi, lo], axis=0)
    for j in range(4):
        loads[1 + j].wait()
        r1 = dot(both, w1[j, 0])
        r = r1[:64] + r1[64:] + dot(hi, w1[j, 1])
        r = r.reshape(4, 2, 8, 512)
        for half in range(2):
            c, s = r[..., 128 * half : 128 * half + 128], r[..., 256 + 128 * half : 384 + 128 * half]
            v = [c[b, 0] + s[b, 1] for b in range(4)] + [c[b, 1] - s[b, 0] for b in range(4)]
            for i, y in enumerate(swap_blocks(v)):
                d = 16 * j + 8 * half + i
                tx1[8 * d : 8 * d + 8, :] = y
    loads[5].wait()
    own = bias[...].astype(F32)
    level[0:8, :] = jnp.concatenate([own, own], axis=1)

    await_all(HARMS + NROW - 2)
    spread("row", NROW, tx1, rx1, send.at[0], recv.at[0])
    swap = pltpu.make_async_remote_copy(
        src_ref=level.at[pl.ds(0, 8), :],
        dst_ref=level.at[pl.ds(8, 8), :],
        send_sem=send.at[4],
        recv_sem=recv.at[4],
        device_id={"harm": harm + 1 - 2 * zhi},
        device_id_type=MESH,
    )
    swap.start()
    for c in loads[6:]:
        c.wait()
    settle(NROW, tx1, rx1, send.at[0], recv.at[0])

    def rows_forward(t, carry):
        hi, lo = split(rx1[pl.ds(t, 64, stride=8), :])
        r = dot(jnp.concatenate([hi, lo, hi], axis=0), e2[t], 0, 0)
        p, q = r[:, :128], r[:, 128:]
        zb[t, 0] = p[:64] + q[64:]
        zb[t, 1] = p[64:] - q[:64]
        return carry

    lax.fori_loop(0, 8, rows_forward, 0)

    def combine(i, carry):
        at = pl.ds(pl.multiple_of(8 * i, 8), 8)
        z = dft8([(zb[t, 0, at, :], zb[t, 1, at, :]) for t in range(8)], -1)
        for q in range(8):
            zb[q, 0, at, :], zb[q, 1, at, :] = z[q]
        return carry

    lax.fori_loop(0, 8, combine, 0)

    def mix(i, carry):
        b, kh = i // 2, i % 2
        at = pl.ds(pl.multiple_of(8 * kh, 8), 8)
        f = []
        for q in range(8):
            re = im = None
            for c in range(4):
                src = pl.ds(pl.multiple_of(16 * c + 8 * kh, 8), 8)
                sr, si = zb[q, 0, src, :], zb[q, 1, src, :]
                gr = g[b, c, 0, at, 128 * q : 128 * q + 128]
                gi = g[b, c, 1, at, 128 * q : 128 * q + 128]
                x, y = gr * sr - gi * si, gr * si + gi * sr
                re, im = (x, y) if c == 0 else (re + x, im + y)
            f.append((re, im))
        y = dft8(f, 1)
        for t in range(8):
            yb[t, pl.ds(pl.multiple_of(8 * i, 8), 8), :] = y[t][0]
            yb[t, pl.ds(pl.multiple_of(64 + 8 * i, 8), 8), :] = y[t][1]
        return carry

    lax.fori_loop(0, 8, mix, 0)

    def rows_inverse(t, carry):
        hi, lo = split(yb[t])
        r = dot(e3[t], jnp.concatenate([hi, lo, hi], axis=1), 1, 1)
        turned = pltpu.roll(r[64:], 64, 1)
        left = lanes_of(turned.shape) < 64
        tx2[pl.ds(t, 64, stride=8), :] = r[:64] + jnp.where(left, -turned, turned)
        return carry

    lax.fori_loop(0, 8, rows_inverse, 0)
    spread("row", NROW, tx2, rx2, send.at[1], recv.at[1])
    settle(NROW, tx2, rx2, send.at[1], recv.at[1])

    for j in range(8):
        v = swap_blocks([rx2[64 * j + 8 * i : 64 * j + 8 * i + 8, :] for i in range(8)])
        for i in range(8):
            xk[8 * i : 8 * i + 8, 128 * j : 128 * j + 128] = v[i]
    hi, lo = split(xk[...])
    both = jnp.concatenate([hi, lo], axis=0)

    def columns_inverse(i, carry):
        u = lax.rem(x + 1 + i, 4)
        r1 = dot(both, w4[u, 0])
        r = r1[:64] + r1[64:] + dot(hi, w4[u, 1])
        fields = (r[:32, :128] - r[32:, 128:], r[32:, :128] + r[:32, 128:])
        at = pl.ds(pl.multiple_of(128 * u, 128), 128)
        for p in range(2):
            acc = None
            for b in range(4):
                y = fields[p][8 * b : 8 * b + 8] + inc[b, p, :, at]
                tot[b, p, :, at] = y
                acc = pw[b] * y if b == 0 else acc + pw[b] * y
            hs[pl.ds(pl.multiple_of(16 * u + 8 * p, 8), 8), :] = acc
        for z in range(2):
            pass_on(rows16(hs, u), rows16(hr, harm), 2 * u + lax.rem(z + 1 + zhi, 2), harm, send.at[2], recv.at[2])
        return carry

    lax.fori_loop(0, 4, columns_inverse, 0)
    swap.wait()
    left = lanes_of((8, 128)) < 64
    own, other = level[0:8, :], level[8:16, :]
    cap = 0.05 + 0.02 * jnp.where(left == (zhi == 0), own, other)
    finish(112, hr, hr, send.at[2], recv.at[2])

    volts = [(hr[16 * h : 16 * h + 8, :], hr[16 * h + 8 : 16 * h + 16, :]) for h in range(HARMS)]
    conduct, charge = [], []
    for w in waves(volts):
        conduct.append(0.05 * (jnp.exp(w * 0.25) - 1.0))
        charge.append(cap * (w + 0.2 * w * w))
    for z in range(2):

        @pl.when(zhi == z)
        def _():
            numbers = [2 * i + z + 1 for i in range(4)]
            for i, (k, (cc, cn), (qc, qn)) in enumerate(
                zip(numbers, harmonics(conduct, numbers), harmonics(charge, numbers))
            ):
                ds[16 * i : 16 * i + 8, :] = cc + (0.25 * k) * qn
                ds[16 * i + 8 : 16 * i + 16, :] = (0.25 * k) * qc - cn

    def hand_back(i, carry):
        to = lax.rem(x + 1 + i, 4)
        pass_on(rows16(ds, to), rows16(dr, x), 2 * to + zhi, harm, send.at[3], recv.at[3])
        return carry

    lax.fori_loop(0, 4, hand_back, 0)
    finish(48, ds, dr, send.at[3], recv.at[3])
    for u in range(4):
        at = slice(128 * u, 128 * u + 128)
        for b in range(4):
            for p in range(2):
                out[b, p, :, at] = tot[b, p, :, at] - pw[b] * dr[16 * u + 8 * p : 16 * u + 8 * p + 8, :]


def body(currents, incident, green, port_weights, bias_level):
    w1, e2, e3, w4 = (jnp.asarray(t) for t in tables())
    vmem = pl.BlockSpec(memory_space=pltpu.VMEM)
    anyw = pl.BlockSpec(memory_space=pl.ANY)
    out = pl.pallas_call(
        kernel,
        out_shape=jax.ShapeDtypeStruct((4, 2, 8, 512), F32),
        in_specs=[anyw] * 9,
        out_specs=vmem,
        scratch_shapes=[
            pltpu.VMEM((4, 2, 8, 512), F32),
            pltpu.VMEM((4, 2, 8, 512), F32),
            pltpu.VMEM((8, 64), jnp.int32),
            pltpu.SMEM((4,), F32),
            pltpu.VMEM((4, 4, 2, 16, 1024), F32),
            pltpu.VMEM(w1.shape, BF16),
            pltpu.VMEM(e2.shape, BF16),
            pltpu.VMEM(e3.shape, BF16),
            pltpu.VMEM(w4.shape, BF16),
            pltpu.VMEM((512, 128), F32),
            pltpu.VMEM((512, 128), F32),
            pltpu.VMEM((8, 2, 64, 128), F32),
            pltpu.VMEM((8, 128, 128), F32),
            pltpu.VMEM((512, 128), F32),
            pltpu.VMEM((512, 128), F32),
            pltpu.VMEM((64, 1024), F32),
            pltpu.VMEM((4, 2, 8, 512), F32),
            pltpu.VMEM((16, 128), F32),
            pltpu.VMEM((64, 128), F32),
            pltpu.VMEM((128, 128), F32),
            pltpu.VMEM((64, 128), F32),
            pltpu.VMEM((64, 128), F32),
            pltpu.SemaphoreType.DMA((12,)),
            pltpu.SemaphoreType.DMA((5,)),
            pltpu.SemaphoreType.DMA((5,)),
        ],
        compiler_params=pltpu.CompilerParams(
            collective_id=0, has_side_effects=True, vmem_limit_bytes=60 * 2**20
        ),
        cost_estimate=pl.CostEstimate(flops=5 * 10**9, bytes_accessed=13 * 10**6, transcendentals=16384),
    )(currents[0], incident[0], bias_level, port_weights, green[0], w1, e2, e3, w4)
    return out[None]


def solution(mesh):
    placed = (
        P("harm", None, None, "row", None),
        P("harm", None, None, "row", None),
        P("harm", None, None, None, "row", None),
        P(),
        P("row", "harm"),
    )
    return jax.shard_map(
        body,
        mesh=mesh,
        in_specs=placed,
        out_specs=P("harm", None, None, "row", None),
        check_vma=False,
    )
```

```python
import functools
import math

import jax
import jax.numpy as jnp
import ml_dtypes
import numpy as np
from jax import lax
from jax.experimental import pallas as pl
from jax.experimental.pallas import tpu as pltpu
from jax.sharding import PartitionSpec as P

MESH = pl.DeviceIdType.MESH
F32 = jnp.float32
BF16 = jnp.bfloat16
HARMS = 8
SAMPLES = 32
NROW = 64
PAD = 1024


def split_np(table):
    high = table.astype(ml_dtypes.bfloat16)
    low = (table - high.astype(np.float64)).astype(ml_dtypes.bfloat16)
    return high, low


def cos_sin(product, length):
    angle = 2.0 * np.pi / length * (product % length).astype(np.float64)
    return np.cos(angle), np.sin(angle)


@functools.lru_cache(maxsize=None)
def tables():
    freq = np.arange(PAD).reshape(4, 16, 2, 8).transpose(0, 2, 1, 3).reshape(4, 2, 128)
    c, s = cos_sin(np.arange(512)[None, :, None] * freq.reshape(4, 1, 256), PAD)
    w1 = np.stack(split_np(np.concatenate([c, s], axis=2)), axis=1)
    r = 8 * np.arange(64)[None, :, None] + np.arange(4)[:, None, None]
    c, s = cos_sin(r * np.arange(128)[None, None, :], PAD)
    hi, lo = split_np(np.concatenate([c, s], axis=2))
    e2 = np.concatenate([hi, hi, lo], axis=1)
    hi, lo = split_np(np.concatenate([c, s], axis=1) / float(PAD * PAD))
    e3 = np.concatenate([hi, hi, lo], axis=2)
    freq = freq.transpose(1, 0, 2).reshape(2, 1, 512, 1)
    c, s = cos_sin(freq * np.arange(512).reshape(1, 4, 1, 128), PAD)
    w4 = np.stack(split_np(np.concatenate([c, s], axis=3)), axis=2)
    c, s = cos_sin(4 * np.arange(128), PAD)
    turn = np.zeros((8, 128), np.float32)
    turn[0], turn[1] = c, s
    return w1, e2, e3, w4, turn


def dft8(z, sign):
    def add(a, b):
        return (a[0] + b[0], a[1] + b[1])

    def sub(a, b):
        return (a[0] - b[0], a[1] - b[1])

    def turn(a):
        return (-a[1], a[0]) if sign > 0 else (a[1], -a[0])

    def four(a0, a1, a2, a3):
        p, m = add(a0, a2), sub(a0, a2)
        q, d = add(a1, a3), turn(sub(a1, a3))
        return [add(p, q), add(m, d), sub(p, q), sub(m, d)]

    even = four(z[0], z[2], z[4], z[6])
    odd = four(z[1], z[3], z[5], z[7])
    h = math.sqrt(0.5)
    o1, o3 = turn(odd[1]), turn(odd[3])
    odd = [
        odd[0],
        ((odd[1][0] + o1[0]) * h, (odd[1][1] + o1[1]) * h),
        turn(odd[2]),
        ((o3[0] - odd[3][0]) * h, (o3[1] - odd[3][1]) * h),
    ]
    return [add(e, o) for e, o in zip(even, odd)] + [sub(e, o) for e, o in zip(even, odd)]


def split(x):
    high = x.astype(BF16)
    return high, (x - high.astype(F32)).astype(BF16)


def lanes_of(shape):
    return lax.broadcasted_iota(jnp.int32, shape, 1)


def swap_blocks(v):
    lane = lanes_of((8, 128))
    stay = (lax.broadcasted_iota(jnp.int32, (8, 128), 0) < 4) == (lane < 64)
    v = [jnp.where(stay, x, pltpu.roll(pltpu.roll(x, 4, 0), 64, 1)) for x in v]
    for bit in (4, 2, 1):
        shift = 8 * bit
        keep = (lane & shift) == 0
        for a in range(8):
            if a & bit:
                continue
            x, y = v[a], v[a + bit]
            v[a] = jnp.where(keep, x, pltpu.roll(y, shift, 1))
            v[a + bit] = jnp.where(keep, pltpu.roll(x, 128 - shift, 1), y)
    return v


def dot(a, b, ca=1, cb=0):
    return lax.dot_general(a, b, (((ca,), (cb,)), ((), ())), preferred_element_type=F32)


def slot(d):
    return 64 * (d // 16) + 8 * lax.rem(d, 8) + 4 * lax.rem(d // 8, 2)


def ordered(d):
    return 4 * d


def rows4(ref, half, at):
    return ref.at[pl.ds(pl.multiple_of(256 * half + at, 4), 4), :]


def spread(half, src, from_slot, dst, to_slot, send, recv):
    me = lax.axis_index("row")
    here = to_slot(me)

    def step(i, carry):
        to = lax.rem(me + i, NROW)
        pltpu.make_async_remote_copy(
            src_ref=rows4(src, half, from_slot(to)),
            dst_ref=rows4(dst, half, here),
            send_sem=send,
            recv_sem=recv,
            device_id={"row": to},
            device_id_type=MESH,
        ).start()
        return carry

    lax.fori_loop(1, NROW, step, 0)
    rows4(dst, half, here)[...] = rows4(src, half, from_slot(me))[...]


def settle(ref, count, sem):
    rows = pl.ds(0, count)
    pltpu.make_async_copy(ref.at[rows], ref.at[rows], sem).wait()


def greet(axis, count):
    me = lax.axis_index(axis)

    def step(i, carry):
        pl.semaphore_signal(
            pltpu.get_barrier_semaphore(),
            inc=1,
            device_id={axis: lax.rem(me + i, count)},
            device_id_type=MESH,
        )
        return carry

    lax.fori_loop(1, count, step, 0)


def await_all(count):
    pl.semaphore_wait(pltpu.get_barrier_semaphore(), count)


def rows16(ref, i):
    return ref.at[pl.ds(pl.multiple_of(16 * i, 16), 16), :]


def pass_on(src, dst, to, harm, send, recv):
    @pl.when(to != harm)
    def _():
        pltpu.make_async_remote_copy(
            src_ref=src,
            dst_ref=dst,
            send_sem=send,
            recv_sem=recv,
            device_id={"harm": to},
            device_id_type=MESH,
        ).start()

    @pl.when(to == harm)
    def _():
        dst[...] = src[...]


def trig(k, n):
    angle = 2.0 * math.pi * ((k * n) % SAMPLES) / SAMPLES
    return math.cos(angle), math.sin(angle)


def waves(volts):
    out = [None] * SAMPLES
    for n in range(9):
        sums = [None] * 4
        for h in range(HARMS):
            c, s = trig(h + 1, n)
            for i, x in (((h + 1) % 2, volts[h][0] * c), (2 + (h + 1) % 2, volts[h][1] * s)):
                sums[i] = x if sums[i] is None else sums[i] + x
        ce, co, se, so = sums
        p, m, u, v = ce + co, ce - co, se + so, se - so
        out[n] = p - u
        out[16 + n] = m - v
        if n:
            out[16 - n] = m + v
            out[SAMPLES - n] = p + u
    return out


def harmonics(x, numbers):
    sums = [[None, None] for _ in numbers]
    odd = numbers[0] % 2
    for n in range(9):
        if n in (0, 8):
            a, d = x[n], x[16 + n]
            even, flat = (a - d, a - d) if odd else (a + d, a + d)
        else:
            a, b, c, d = x[n], x[SAMPLES - n], x[16 - n], x[16 + n]
            even = (a + b) - (c + d) if odd else (a + b) + (c + d)
            flat = (a - b) + (c - d) if odd else (a - b) - (c - d)
        for i, k in enumerate(numbers):
            for part, (y, w) in enumerate(zip((even, flat), trig(k, n))):
                if abs(w) < 1e-12:
                    continue
                y = y * (w * 2.0 / SAMPLES)
                sums[i][part] = y if sums[i][part] is None else sums[i][part] + y
    return sums


def kernel(
    cur_hbm, inc_hbm, bias_hbm, pw_hbm, turn_hbm, g_hbm, w1_hbm, e2_hbm, e3_hbm, w4_hbm, out,
    cur, inc, bias, pw, turn, g, w1, e2, e3, w4, tx1, rx1, zb, yb, tx2, rx2, xk, part, tot,
    level, hs, hr, ds, dr, load, send, recv,
):
    harm = lax.axis_index("harm")
    x, zhi = harm // 2, lax.rem(harm, 2)
    greet("harm", HARMS)
    greet("row", NROW)
    pairs = [(cur_hbm, cur)] + [(w1_hbm.at[j], w1.at[j]) for j in range(4)]
    pairs += [(bias_hbm, bias), (pw_hbm, pw), (turn_hbm, turn), (e2_hbm, e2), (g_hbm, g), (e3_hbm, e3)]
    pairs += [(inc_hbm, inc), (w4_hbm, w4)]
    loads = [pltpu.make_async_copy(a, b, load.at[i]) for i, (a, b) in enumerate(pairs)]
    for c in loads:
        c.start()

    loads[0].wait()
    hi, lo = split(cur[...].reshape(64, 512))
    both = jnp.concatenate([hi, lo], axis=0)
    for j in range(4):
        loads[1 + j].wait()
        r1 = dot(both, w1[j, 0])
        r = r1[:64] + r1[64:] + dot(hi, w1[j, 1])
        r = r.reshape(4, 2, 8, 512)
        for half in range(2):
            c, s = r[..., 128 * half : 128 * half + 128], r[..., 256 + 128 * half : 384 + 128 * half]
            v = [c[b, 0] + s[b, 1] for b in range(4)] + [c[b, 1] - s[b, 0] for b in range(4)]
            for i, y in enumerate(swap_blocks(v)):
                at = 256 * half + 64 * j + 8 * i
                tx1[at : at + 8, :] = y
    loads[5].wait()
    own = bias[...].astype(F32)
    level[0:8, :] = jnp.concatenate([own, own], axis=1)

    await_all(HARMS + NROW - 2)
    for half in range(2):
        spread(half, tx1, slot, rx1, ordered, send.at[half], recv.at[half])
    swap = pltpu.make_async_remote_copy(
        src_ref=level.at[pl.ds(0, 8), :],
        dst_ref=level.at[pl.ds(8, 8), :],
        send_sem=send.at[6],
        recv_sem=recv.at[6],
        device_id={"harm": harm + 1 - 2 * zhi},
        device_id_type=MESH,
    )
    swap.start()
    for c in loads[6:11]:
        c.wait()
    tc, ts = turn[0:1, :], turn[1:2, :]
    inner = (lanes_of((64, 128)) & 32) == 0

    for half in range(2):
        settle(rx1, 252, recv.at[half])
        for t in range(4):
            hi, lo = split(rx1[pl.ds(256 * half + t, 64, stride=4), :])
            r = dot(jnp.concatenate([hi, lo, hi], axis=0), e2[t], 0, 0)
            p, q = r[:, :128], r[:, 128:]
            zb[t, 0], zb[t, 1] = p[:32] + q[32:64], p[32:64] - q[:32]
            re, im = p[64:96] + q[96:], p[96:] - q[64:96]
            zb[4 + t, 0], zb[4 + t, 1] = re * tc + im * ts, im * tc - re * ts
        for c in range(4):
            at = slice(8 * c, 8 * c + 8)
            z = dft8([(zb[t, 0, at, :], zb[t, 1, at, :]) for t in range(8)], -1)
            for q in range(8):
                zb[q, 0, at, :], zb[q, 1, at, :] = z[q]

        def mix(b, carry):
            f = []
            for q in range(8):
                re = im = None
                for c in range(4):
                    sr, si = zb[q, 0, 8 * c : 8 * c + 8, :], zb[q, 1, 8 * c : 8 * c + 8, :]
                    gr, gi = (
                        g[b, c, p, 8 * half : 8 * half + 8, 128 * q : 128 * q + 128] for p in range(2)
                    )
                    u, w = gr * sr - gi * si, gr * si + gi * sr
                    re, im = (u, w) if c == 0 else (re + u, im + w)
                f.append((re, im))
            y = dft8(f, 1)
            for t in range(4):
                (ar, ai), (br, bi) = y[t], y[4 + t]
                for p, w in enumerate((ar, ai, br * tc - bi * ts, bi * tc + br * ts)):
                    yb[t, pl.ds(pl.multiple_of(32 * p + 8 * b, 8), 8), :] = w
            return carry

        lax.fori_loop(0, 4, mix, 0)
        for t in range(4):
            hi, lo = split(yb[t])
            r = dot(e3[t], jnp.concatenate([hi, lo, hi], axis=1), 1, 1)
            s = r[64:]
            turned = jnp.where(inner, -pltpu.roll(s, 96, 1), pltpu.roll(s, 32, 1))
            tx2[pl.ds(256 * half + t, 64, stride=4), :] = r[:64] + turned
        spread(half, tx2, ordered, rx2, slot, send.at[2 + half], recv.at[2 + half])

    for c in loads[11:]:
        c.wait()
    for half in range(2):
        settle(rx2, 252, recv.at[2 + half])
        for j in range(4):
            at = 256 * half + 64 * j
            v = swap_blocks([rx2[at + 8 * i : at + 8 * i + 8, :] for i in range(8)])
            for i in range(8):
                xk[8 * i : 8 * i + 8, 128 * j : 128 * j + 128] = v[i]
        hi, lo = split(xk[...])
        both = jnp.concatenate([hi, lo], axis=0)
        if half == 0:
            for u in range(4):
                r1 = dot(both, w4[0, u, 0])
                part[u] = r1[:64] + r1[64:] + dot(hi, w4[0, u, 1])

    def columns_inverse(i, carry):
        u = lax.rem(x + 1 + i, 4)
        r1 = dot(both, w4[1, u, 0])
        r = r1[:64] + r1[64:] + dot(hi, w4[1, u, 1]) + part[u]
        fields = (r[:32, :128] - r[32:, 128:], r[32:, :128] + r[:32, 128:])
        at = pl.ds(pl.multiple_of(128 * u, 128), 128)
        for p in range(2):
            acc = None
            for b in range(4):
                y = fields[p][8 * b : 8 * b + 8] + inc[b, p, :, at]
                tot[b, p, :, at] = y
                acc = pw[b] * y if b == 0 else acc + pw[b] * y
            hs[pl.ds(pl.multiple_of(16 * u + 8 * p, 8), 8), :] = acc
        for z in range(2):
            pass_on(rows16(hs, u), rows16(hr, harm), 2 * u + lax.rem(z + 1 + zhi, 2), harm, send.at[4], recv.at[4])
        return carry

    lax.fori_loop(0, 4, columns_inverse, 0)
    swap.wait()
    left = lanes_of((8, 128)) < 64
    own, other = level[0:8, :], level[8:16, :]
    cap = 0.05 + 0.02 * jnp.where(left == (zhi == 0), own, other)
    settle(hr, 112, recv.at[4])

    volts = [(hr[16 * h : 16 * h + 8, :], hr[16 * h + 8 : 16 * h + 16, :]) for h in range(HARMS)]
    conduct, charge = [], []
    for w in waves(volts):
        conduct.append(0.05 * (jnp.exp(w * 0.25) - 1.0))
        charge.append(cap * (w + 0.2 * w * w))
    for z in range(2):

        @pl.when(zhi == z)
        def _():
            numbers = [2 * i + z + 1 for i in range(4)]
            for i, (k, (cc, cn), (qc, qn)) in enumerate(
                zip(numbers, harmonics(conduct, numbers), harmonics(charge, numbers))
            ):
                ds[16 * i : 16 * i + 8, :] = cc + (0.25 * k) * qn
                ds[16 * i + 8 : 16 * i + 16, :] = (0.25 * k) * qc - cn

    def hand_back(i, carry):
        to = lax.rem(x + 1 + i, 4)
        pass_on(rows16(ds, to), rows16(dr, x), 2 * to + zhi, harm, send.at[5], recv.at[5])
        return carry

    lax.fori_loop(0, 4, hand_back, 0)
    settle(dr, 48, recv.at[5])
    for u in range(4):
        at = slice(128 * u, 128 * u + 128)
        for b in range(4):
            for p in range(2):
                out[b, p, :, at] = tot[b, p, :, at] - pw[b] * dr[16 * u + 8 * p : 16 * u + 8 * p + 8, :]
    for i in range(4):
        settle((tx1, tx1, tx2, tx2)[i], 252, send.at[i])
    settle(hr, 112, send.at[4])
    settle(ds, 48, send.at[5])


def body(currents, incident, green, port_weights, bias_level):
    w1, e2, e3, w4, turn = (jnp.asarray(t) for t in tables())
    vmem = pl.BlockSpec(memory_space=pltpu.VMEM)
    anyw = pl.BlockSpec(memory_space=pltpu.HBM)
    out = pl.pallas_call(
        kernel,
        out_shape=jax.ShapeDtypeStruct((4, 2, 8, 512), F32),
        in_specs=[anyw] * 10,
        out_specs=vmem,
        scratch_shapes=[
            pltpu.VMEM((4, 2, 8, 512), F32),
            pltpu.VMEM((4, 2, 8, 512), F32),
            pltpu.VMEM((8, 64), jnp.int32),
            pltpu.SMEM((4,), F32),
            pltpu.VMEM((8, 128), F32),
            pltpu.VMEM((4, 4, 2, 16, 1024), F32),
            pltpu.VMEM(w1.shape, BF16),
            pltpu.VMEM(e2.shape, BF16),
            pltpu.VMEM(e3.shape, BF16),
            pltpu.VMEM(w4.shape, BF16),
            pltpu.VMEM((512, 128), F32),
            pltpu.VMEM((512, 128), F32),
            pltpu.VMEM((8, 2, 32, 128), F32),
            pltpu.VMEM((4, 128, 128), F32),
            pltpu.VMEM((512, 128), F32),
            pltpu.VMEM((512, 128), F32),
            pltpu.VMEM((64, 512), F32),
            pltpu.VMEM((4, 64, 256), F32),
            pltpu.VMEM((4, 2, 8, 512), F32),
            pltpu.VMEM((16, 128), F32),
            pltpu.VMEM((64, 128), F32),
            pltpu.VMEM((128, 128), F32),
            pltpu.VMEM((64, 128), F32),
            pltpu.VMEM((64, 128), F32),
            pltpu.SemaphoreType.DMA((13,)),
            pltpu.SemaphoreType.DMA((7,)),
            pltpu.SemaphoreType.DMA((7,)),
        ],
        compiler_params=pltpu.CompilerParams(
            collective_id=0, has_side_effects=True, vmem_limit_bytes=60 * 2**20
        ),
        cost_estimate=pl.CostEstimate(flops=5 * 10**9, bytes_accessed=13 * 10**6, transcendentals=16384),
    )(currents[0], incident[0], bias_level, port_weights, turn, green[0], w1, e2, e3, w4)
    return out[None]


def solution(mesh):
    placed = (
        P("harm", None, None, "row", None),
        P("harm", None, None, "row", None),
        P("harm", None, None, None, "row", None),
        P(),
        P("row", "harm"),
    )
    return jax.shard_map(
        body,
        mesh=mesh,
        in_specs=placed,
        out_specs=P("harm", None, None, "row", None),
        check_vma=False,
    )
```

```python
import functools
import math

import jax
import jax.numpy as jnp
import ml_dtypes
import numpy as np
from jax import lax
from jax.experimental import pallas as pl
from jax.experimental.pallas import tpu as pltpu
from jax.sharding import PartitionSpec as P

MESH = pl.DeviceIdType.MESH
F32 = jnp.float32
BF16 = jnp.bfloat16
HARMS = 8
SAMPLES = 32
NROW = 64
PAD = 1024


def split_np(table):
    high = table.astype(ml_dtypes.bfloat16)
    low = (table - high.astype(np.float64)).astype(ml_dtypes.bfloat16)
    return high, low


def cos_sin(product, length):
    angle = 2.0 * np.pi / length * (product % length).astype(np.float64)
    return np.cos(angle), np.sin(angle)


@functools.lru_cache(maxsize=None)
def tables():
    freq = np.arange(PAD).reshape(4, 16, 2, 8).transpose(0, 2, 1, 3).reshape(4, 2, 128)
    c, s = cos_sin(np.arange(512)[None, :, None] * freq.reshape(4, 1, 256), PAD)
    w1 = np.stack(split_np(np.concatenate([c, s], axis=2)), axis=1)
    r = 8 * np.arange(64)[None, :, None] + np.arange(4)[:, None, None]
    c, s = cos_sin(r * np.arange(128)[None, None, :], PAD)
    hi, lo = split_np(np.concatenate([c, s], axis=2))
    e2 = np.concatenate([hi, hi, lo], axis=1)
    c, s = cos_sin(8 * np.arange(64)[:, None] * np.arange(128)[None, :], PAD)
    hi, lo = split_np(np.concatenate([c, s], axis=0) / float(PAD * PAD))
    e3 = np.concatenate([hi, hi, lo], axis=1)
    freq = np.arange(PAD).reshape(64, 2, 8).transpose(1, 2, 0).reshape(2, 1, 512, 1)
    c, s = cos_sin(freq * np.arange(512).reshape(1, 4, 1, 128), PAD)
    w4 = np.stack(split_np(np.concatenate([c, s], axis=3)), axis=2)
    turn = np.concatenate(cos_sin(np.arange(8)[:, None] * np.arange(128)[None, :], PAD)).astype(np.float32)
    return w1, e2, e3, w4, turn


def dft8(z, sign):
    def add(a, b):
        return (a[0] + b[0], a[1] + b[1])

    def sub(a, b):
        return (a[0] - b[0], a[1] - b[1])

    def turn(a):
        return (-a[1], a[0]) if sign > 0 else (a[1], -a[0])

    def four(a0, a1, a2, a3):
        p, m = add(a0, a2), sub(a0, a2)
        q, d = add(a1, a3), turn(sub(a1, a3))
        return [add(p, q), add(m, d), sub(p, q), sub(m, d)]

    even = four(z[0], z[2], z[4], z[6])
    odd = four(z[1], z[3], z[5], z[7])
    h = math.sqrt(0.5)
    o1, o3 = turn(odd[1]), turn(odd[3])
    odd = [
        odd[0],
        ((odd[1][0] + o1[0]) * h, (odd[1][1] + o1[1]) * h),
        turn(odd[2]),
        ((o3[0] - odd[3][0]) * h, (o3[1] - odd[3][1]) * h),
    ]
    return [add(e, o) for e, o in zip(even, odd)] + [sub(e, o) for e, o in zip(even, odd)]


def split(x):
    high = x.astype(BF16)
    return high, (x - high.astype(F32)).astype(BF16)


def lanes_of(shape):
    return lax.broadcasted_iota(jnp.int32, shape, 1)


def swap_blocks(v):
    lane = lanes_of((8, 128))
    stay = (lax.broadcasted_iota(jnp.int32, (8, 128), 0) < 4) == (lane < 64)
    v = [jnp.where(stay, x, pltpu.roll(pltpu.roll(x, 4, 0), 64, 1)) for x in v]
    for bit in (4, 2, 1):
        shift = 8 * bit
        keep = (lane & shift) == 0
        for a in range(8):
            if a & bit:
                continue
            x, y = v[a], v[a + bit]
            v[a] = jnp.where(keep, x, pltpu.roll(y, shift, 1))
            v[a + bit] = jnp.where(keep, pltpu.roll(x, 128 - shift, 1), y)
    return v


def to_rows(x, y, ref):
    ref[...] = jnp.concatenate([x, y], axis=0).T
    left = lanes_of((16, 128)) < 64
    first, second = [], []
    for i in range(4):
        p, q = (ref[pl.ds(2 * i + j, 16, stride=8), :] for j in range(2))
        first.append(jnp.where(left, p, pltpu.roll(q, 64, 1)))
        second.append(jnp.where(left, pltpu.roll(p, 64, 1), q))
    return jnp.concatenate(first, axis=1), jnp.concatenate(second, axis=1)


def to_columns(x, w, u):
    hi, lo = split(x)
    rows = x.shape[0]
    r = dot(jnp.concatenate([hi, lo], axis=0), w[u, 0])
    return r[:rows] + r[rows:] + dot(hi, w[u, 1])


def parts(r):
    return r[:8, :128] - r[8:, 128:], r[8:, :128] + r[:8, 128:]


def dot(a, b, ca=1, cb=0):
    return lax.dot_general(a, b, (((ca,), (cb,)), ((), ())), preferred_element_type=F32)


def rows_at(ref, count, at):
    if count > 1:
        at = pl.multiple_of(at, 2 if count == 2 else 8)
    return ref.at[pl.ds(at, count), :]


def spread(count, src, place, dst, here, send, recv):
    me = lax.axis_index("row")

    def step(i, carry):
        to = lax.rem(me + i, NROW)
        pltpu.make_async_remote_copy(
            src_ref=rows_at(src, count, place(to)),
            dst_ref=rows_at(dst, count, here),
            send_sem=send,
            recv_sem=recv,
            device_id={"row": to},
            device_id_type=MESH,
        ).start()
        return carry

    lax.fori_loop(1, NROW, step, 0)
    rows_at(dst, count, here)[...] = rows_at(src, count, place(me))[...]


def settle(ref, count, sem):
    rows = pl.ds(0, count)
    pltpu.make_async_copy(ref.at[rows], ref.at[rows], sem).wait()


def greet(axis, count):
    me = lax.axis_index(axis)

    def step(i, carry):
        pl.semaphore_signal(
            pltpu.get_barrier_semaphore(),
            inc=1,
            device_id={axis: me ^ (count - i)},
            device_id_type=MESH,
        )
        return carry

    lax.fori_loop(1, count, step, 0)


def await_all(count):
    pl.semaphore_wait(pltpu.get_barrier_semaphore(), count)


def rows16(ref, i):
    return ref.at[pl.ds(pl.multiple_of(16 * i, 16), 16), :]


def pass_on(src, dst, to, harm, send, recv):
    @pl.when(to != harm)
    def _():
        pltpu.make_async_remote_copy(
            src_ref=src,
            dst_ref=dst,
            send_sem=send,
            recv_sem=recv,
            device_id={"harm": to},
            device_id_type=MESH,
        ).start()

    @pl.when(to == harm)
    def _():
        dst[...] = src[...]


def trig(k, n):
    angle = 2.0 * math.pi * ((k * n) % SAMPLES) / SAMPLES
    return math.cos(angle), math.sin(angle)


def waves(volts):
    out = [None] * SAMPLES
    for n in range(9):
        sums = [None] * 4
        for h in range(HARMS):
            c, s = trig(h + 1, n)
            for i, x in (((h + 1) % 2, volts[h][0] * c), (2 + (h + 1) % 2, volts[h][1] * s)):
                sums[i] = x if sums[i] is None else sums[i] + x
        ce, co, se, so = sums
        p, m, u, v = ce + co, ce - co, se + so, se - so
        out[n] = p - u
        out[16 + n] = m - v
        if n:
            out[16 - n] = m + v
            out[SAMPLES - n] = p + u
    return out


def harmonics(x, numbers):
    sums = [[None, None] for _ in numbers]
    odd = numbers[0] % 2
    for n in range(9):
        if n in (0, 8):
            a, d = x[n], x[16 + n]
            even, flat = (a - d, a - d) if odd else (a + d, a + d)
        else:
            a, b, c, d = x[n], x[SAMPLES - n], x[16 - n], x[16 + n]
            even = (a + b) - (c + d) if odd else (a + b) + (c + d)
            flat = (a - b) + (c - d) if odd else (a - b) - (c - d)
        for i, k in enumerate(numbers):
            for part, (y, w) in enumerate(zip((even, flat), trig(k, n))):
                if abs(w) < 1e-12:
                    continue
                y = y * (w * 2.0 / SAMPLES)
                sums[i][part] = y if sums[i][part] is None else sums[i][part] + y
    return sums


def kernel(
    cur_hbm, inc_hbm, bias_hbm, pw_hbm, turn_hbm, g_hbm, w1_hbm, e2_hbm, e3_hbm, w4_hbm, out,
    cur, inc, bias, pw, turn, g, w1, e2, e3, w4, tx1, rx1, zb, yb, txv, rxv, txr, rxr, tr, vinc, vf, ff,
    level, hs, hr, ds, dr, load, send, recv,
):
    harm = lax.axis_index("harm")
    x, zhi = harm // 2, lax.rem(harm, 2)
    greet("harm", HARMS)
    greet("row", NROW)
    pairs = [(cur_hbm, cur)] + [(w1_hbm.at[j], w1.at[j]) for j in range(4)]
    pairs += [(bias_hbm, bias), (pw_hbm, pw), (turn_hbm, turn), (e2_hbm, e2), (g_hbm, g), (e3_hbm, e3)]
    pairs += [(inc_hbm, inc), (w4_hbm, w4)]
    loads = [pltpu.make_async_copy(a, b, load.at[i]) for i, (a, b) in enumerate(pairs)]
    for c in loads:
        c.start()

    loads[0].wait()
    hi, lo = split(cur[...].reshape(64, 512))
    both = jnp.concatenate([hi, lo], axis=0)
    for j in range(4):
        loads[1 + j].wait()
        r1 = dot(both, w1[j, 0])
        r = r1[:64] + r1[64:] + dot(hi, w1[j, 1])
        r = r.reshape(4, 2, 8, 512)
        for half in range(2):
            c, s = r[..., 128 * half : 128 * half + 128], r[..., 256 + 128 * half : 384 + 128 * half]
            v = [c[b, 0] + s[b, 1] for b in range(4)] + [c[b, 1] - s[b, 0] for b in range(4)]
            for i, y in enumerate(swap_blocks(v)):
                at = 8 * (16 * j + i) + 4 * half
                tx1[at : at + 4, :] = y[:4]
                tx1[at + 64 : at + 68, :] = y[4:]
    loads[5].wait()
    own = bias[...].astype(F32)
    level[0:8, :] = jnp.concatenate([own, own], axis=1)

    row = lax.axis_index("row")
    await_all(HARMS + NROW - 2)
    spread(8, tx1, lambda d: 8 * d, rx1, 8 * row, send.at[0], recv.at[0])
    swap = pltpu.make_async_remote_copy(
        src_ref=level.at[pl.ds(0, 8), :],
        dst_ref=level.at[pl.ds(8, 8), :],
        send_sem=send.at[5],
        recv_sem=recv.at[5],
        device_id={"harm": harm + 1 - 2 * zhi},
        device_id_type=MESH,
    )
    swap.start()
    for c in loads[6:]:
        c.wait()
    for p in range(2):
        vinc[p] = pw[0] * inc[0, p] + pw[1] * inc[1, p] + pw[2] * inc[2, p] + pw[3] * inc[3, p]
    tc = [turn[t : t + 1, :] for t in range(8)]
    ts = [turn[8 + t : 9 + t, :] for t in range(8)]
    left = lanes_of((64, 128)) < 64

    def rows_inverse(i):
        hi, lo = split(yb[i])
        r = dot(e3[...], jnp.concatenate([hi, lo, hi], axis=1), 1, 1)
        s = pltpu.roll(r[64:], 64, 1)
        return r[:64] + jnp.where(left, -s, s)

    settle(rx1, 504, recv.at[0])
    for half in range(2):
        for t in range(4):
            hi, lo = split(rx1[pl.ds(4 * half + t, 64, stride=8), :])
            r = dot(jnp.concatenate([hi, lo, hi], axis=0), e2[t], 0, 0)
            p, q = r[:, :128], r[:, 128:]
            zb[t, 0], zb[t, 1] = p[:32] + q[32:64], p[32:64] - q[:32]
            re, im = p[64:96] + q[96:], p[96:] - q[64:96]
            zb[4 + t, 0], zb[4 + t, 1] = re * tc[4] + im * ts[4], im * tc[4] - re * ts[4]
        for c in range(4):
            at = slice(8 * c, 8 * c + 8)
            z = dft8([(zb[t, 0, at, :], zb[t, 1, at, :]) for t in range(8)], -1)
            for q in range(8):
                zb[q, 0, at, :], zb[q, 1, at, :] = z[q]

        def keep(i, f):
            for t, (re, im) in enumerate(dft8(f, 1)):
                if t:
                    re, im = re * tc[t] - im * ts[t], im * tc[t] + re * ts[t]
                yb[4 * half + i, 8 * t : 8 * t + 8, :] = re
                yb[4 * half + i, 64 + 8 * t : 72 + 8 * t, :] = im

        port = None
        for b in range(4):
            f = []
            for q in range(8):
                re = im = None
                for c in range(4):
                    sr, si = zb[q, 0, 8 * c : 8 * c + 8, :], zb[q, 1, 8 * c : 8 * c + 8, :]
                    gr, gi = (
                        g[b, c, p, 8 * half : 8 * half + 8, 128 * q : 128 * q + 128] for p in range(2)
                    )
                    u, w = gr * sr - gi * si, gr * si + gi * sr
                    re, im = (u, w) if c == 0 else (re + u, im + w)
                f.append((re, im))
            if b < 3:
                keep(b + 1, f)
            terms = [(pw[b] * re, pw[b] * im) for re, im in f]
            port = terms if b == 0 else [(v[0] + w[0], v[1] + w[1]) for v, w in zip(port, terms)]
        keep(0, port)
        txv[pl.ds(half, 64, stride=2), :] = rows_inverse(4 * half)
    spread(2, txv, lambda d: 2 * d, rxv, 2 * row, send.at[1], recv.at[1])
    for half in range(2):
        for i in range(3):
            txr[pl.ds(3 * half + i, 64, stride=8), :] = rows_inverse(4 * half + 1 + i)
    spread(6, txr, lambda d: 8 * d, rxr, 8 * row, send.at[2], recv.at[2])

    def block(i, half):
        return rxr[pl.ds(3 * half + i, 64, stride=8), :]

    settle(rxv, 126, recv.at[1])
    x0, x1 = to_rows(*(rxv[pl.ds(half, 64, stride=2), :] for half in range(2)), tr.at[0])
    for i in range(4):
        u = lax.rem(x + 1 + i, 4)
        at = pl.ds(pl.multiple_of(128 * u, 128), 128)
        for p, y in enumerate(parts(to_columns(x0, w4.at[0], u) + to_columns(x1, w4.at[1], u))):
            vf[p, :, at] = y
            hs[pl.ds(pl.multiple_of(16 * u + 8 * p, 8), 8), :] = y + vinc[p, :, at]
        for z in range(2):
            pass_on(rows16(hs, u), rows16(hr, harm), 2 * u + lax.rem(z + 1 + zhi, 2), harm, send.at[3], recv.at[3])

    settle(rxr, 378, recv.at[2])
    both = [to_rows(block(i, 0), block(i, 1), tr.at[1 + i]) for i in range(3)]
    xa = [jnp.concatenate([both[i][half] for i in range(3)], axis=0) for half in range(2)]
    for u in range(4):
        r = to_columns(xa[0], w4.at[0], u) + to_columns(xa[1], w4.at[1], u)
        for i in range(3):
            for p, y in enumerate(parts(r[16 * i : 16 * i + 16])):
                ff[i, p, :, 128 * u : 128 * u + 128] = y
    swap.wait()
    left = lanes_of((8, 128)) < 64
    own, other = level[0:8, :], level[8:16, :]
    cap = 0.05 + 0.02 * jnp.where(left == (zhi == 0), own, other)
    settle(hr, 112, recv.at[3])

    volts = [(hr[16 * h : 16 * h + 8, :], hr[16 * h + 8 : 16 * h + 16, :]) for h in range(HARMS)]
    conduct, charge = [], []
    for w in waves(volts):
        conduct.append(0.05 * (jnp.exp(w * 0.25) - 1.0))
        charge.append(cap * (w + 0.2 * w * w))
    for z in range(2):

        @pl.when(zhi == z)
        def _():
            numbers = [2 * i + z + 1 for i in range(4)]
            for i, (k, (cc, cn), (qc, qn)) in enumerate(
                zip(numbers, harmonics(conduct, numbers), harmonics(charge, numbers))
            ):
                ds[16 * i : 16 * i + 8, :] = cc + (0.25 * k) * qn
                ds[16 * i + 8 : 16 * i + 16, :] = (0.25 * k) * qc - cn

    def hand_back(i, carry):
        to = lax.rem(x + 1 + i, 4)
        pass_on(rows16(ds, to), rows16(dr, x), 2 * to + zhi, harm, send.at[4], recv.at[4])
        return carry

    lax.fori_loop(0, 4, hand_back, 0)

    last = 1.0 / jnp.full((8, 128), pw[3], F32)
    settle(dr, 48, recv.at[4])
    for u in range(4):
        at = slice(128 * u, 128 * u + 128)
        for p in range(2):
            diode = dr[16 * u + 8 * p : 16 * u + 8 * p + 8, :]
            rest = vf[p, :, at]
            for b in range(3):
                y = ff[b, p, :, at]
                rest = rest - pw[b] * y
                out[b, p, :, at] = y + inc[b, p, :, at] - pw[b] * diode
            out[3, p, :, at] = rest * last + inc[3, p, :, at] - pw[3] * diode
    for i, (ref, count) in enumerate(
        ((tx1, 504), (txv, 126), (txr, 378), (hr, 112), (ds, 48))
    ):
        settle(ref, count, send.at[i])


def body(currents, incident, green, port_weights, bias_level):
    w1, e2, e3, w4, turn = (jnp.asarray(t) for t in tables())
    vmem = pl.BlockSpec(memory_space=pltpu.VMEM)
    anyw = pl.BlockSpec(memory_space=pltpu.HBM)
    out = pl.pallas_call(
        kernel,
        out_shape=jax.ShapeDtypeStruct((4, 2, 8, 512), F32),
        in_specs=[anyw] * 10,
        out_specs=vmem,
        scratch_shapes=[
            pltpu.VMEM((4, 2, 8, 512), F32),
            pltpu.VMEM((4, 2, 8, 512), F32),
            pltpu.VMEM((8, 64), jnp.int32),
            pltpu.SMEM((4,), F32),
            pltpu.VMEM((16, 128), F32),
            pltpu.VMEM((4, 4, 2, 16, 1024), F32),
            pltpu.VMEM(w1.shape, BF16),
            pltpu.VMEM(e2.shape, BF16),
            pltpu.VMEM(e3.shape, BF16),
            pltpu.VMEM(w4.shape, BF16),
            pltpu.VMEM((512, 128), F32),
            pltpu.VMEM((512, 128), F32),
            pltpu.VMEM((8, 2, 32, 128), F32),
            pltpu.VMEM((8, 128, 128), F32),
            pltpu.VMEM((128, 128), F32),
            pltpu.VMEM((128, 128), F32),
            pltpu.VMEM((512, 128), F32),
            pltpu.VMEM((512, 128), F32),
            pltpu.VMEM((4, 128, 128), F32),
            pltpu.VMEM((2, 8, 512), F32),
            pltpu.VMEM((2, 8, 512), F32),
            pltpu.VMEM((3, 2, 8, 512), F32),
            pltpu.VMEM((16, 128), F32),
            pltpu.VMEM((64, 128), F32),
            pltpu.VMEM((128, 128), F32),
            pltpu.VMEM((64, 128), F32),
            pltpu.VMEM((64, 128), F32),
            pltpu.SemaphoreType.DMA((13,)),
            pltpu.SemaphoreType.DMA((6,)),
            pltpu.SemaphoreType.DMA((6,)),
        ],
        compiler_params=pltpu.CompilerParams(
            collective_id=0, has_side_effects=True, vmem_limit_bytes=60 * 2**20
        ),
        cost_estimate=pl.CostEstimate(flops=5 * 10**9, bytes_accessed=13 * 10**6, transcendentals=16384),
    )(currents[0], incident[0], bias_level, port_weights, turn, green[0], w1, e2, e3, w4)
    return out[None]


def solution(mesh):
    placed = (
        P("harm", None, None, "row", None),
        P("harm", None, None, "row", None),
        P("harm", None, None, None, "row", None),
        P(),
        P("row", "harm"),
    )
    return jax.shard_map(
        body,
        mesh=mesh,
        in_specs=placed,
        out_specs=P("harm", None, None, "row", None),
        check_vma=False,
    )
```

```python
import functools
import math

import jax
import jax.numpy as jnp
import ml_dtypes
import numpy as np
from jax import lax
from jax.experimental import pallas as pl
from jax.experimental.pallas import tpu as pltpu
from jax.sharding import PartitionSpec as P

MESH = pl.DeviceIdType.MESH
F32 = jnp.float32
BF16 = jnp.bfloat16
HARMS = 8
SAMPLES = 32
NROW = 64
PAD = 1024


def split_np(table):
    high = table.astype(ml_dtypes.bfloat16)
    low = (table - high.astype(np.float64)).astype(ml_dtypes.bfloat16)
    return high, low


def cos_sin(product, length):
    angle = 2.0 * np.pi / length * (product % length).astype(np.float64)
    return np.cos(angle), np.sin(angle)


@functools.lru_cache(maxsize=None)
def tables():
    freq = np.arange(PAD).reshape(4, 16, 2, 8).transpose(0, 2, 1, 3).reshape(4, 2, 128)
    c, s = cos_sin(np.arange(512)[None, :, None] * freq.reshape(4, 1, 256), PAD)
    w1 = np.stack(split_np(np.concatenate([c, s], axis=2)), axis=1)
    r = 8 * np.arange(64)[None, :, None] + np.arange(4)[:, None, None]
    c, s = cos_sin(r * np.arange(128)[None, None, :], PAD)
    hi, lo = split_np(np.concatenate([c, s], axis=2))
    e2 = np.concatenate([hi, hi, lo], axis=1)
    c, s = cos_sin(8 * np.arange(64)[:, None] * np.arange(128)[None, :], PAD)
    hi, lo = split_np(np.concatenate([c, s], axis=0) / float(PAD * PAD))
    e3 = np.concatenate([hi, hi, lo], axis=1)
    freq = np.arange(PAD).reshape(64, 2, 8).transpose(1, 2, 0).reshape(2, 1, 512, 1)
    c, s = cos_sin(freq * np.arange(512).reshape(1, 4, 1, 128), PAD)
    w4 = np.stack(split_np(np.concatenate([c, s], axis=3)), axis=2)
    turn = np.concatenate(cos_sin(np.arange(8)[:, None] * np.arange(128)[None, :], PAD)).astype(np.float32)
    return w1, e2, e3, w4, turn


def dft8(z, sign):
    def add(a, b):
        return (a[0] + b[0], a[1] + b[1])

    def sub(a, b):
        return (a[0] - b[0], a[1] - b[1])

    def turn(a):
        return (-a[1], a[0]) if sign > 0 else (a[1], -a[0])

    def four(a0, a1, a2, a3):
        p, m = add(a0, a2), sub(a0, a2)
        q, d = add(a1, a3), turn(sub(a1, a3))
        return [add(p, q), add(m, d), sub(p, q), sub(m, d)]

    even = four(z[0], z[2], z[4], z[6])
    odd = four(z[1], z[3], z[5], z[7])
    h = math.sqrt(0.5)
    o1, o3 = turn(odd[1]), turn(odd[3])
    odd = [
        odd[0],
        ((odd[1][0] + o1[0]) * h, (odd[1][1] + o1[1]) * h),
        turn(odd[2]),
        ((o3[0] - odd[3][0]) * h, (o3[1] - odd[3][1]) * h),
    ]
    return [add(e, o) for e, o in zip(even, odd)] + [sub(e, o) for e, o in zip(even, odd)]


def split(x):
    high = x.astype(BF16)
    return high, (x - high.astype(F32)).astype(BF16)


def lanes_of(shape):
    return lax.broadcasted_iota(jnp.int32, shape, 1)


def swap_blocks(v):
    lane = lanes_of((8, 128))
    stay = (lax.broadcasted_iota(jnp.int32, (8, 128), 0) < 4) == (lane < 64)
    v = [jnp.where(stay, x, pltpu.roll(pltpu.roll(x, 4, 0), 64, 1)) for x in v]
    for bit in (4, 2, 1):
        shift = 8 * bit
        keep = (lane & shift) == 0
        for a in range(8):
            if a & bit:
                continue
            x, y = v[a], v[a + bit]
            v[a] = jnp.where(keep, x, pltpu.roll(y, shift, 1))
            v[a + bit] = jnp.where(keep, pltpu.roll(x, 128 - shift, 1), y)
    return v


def to_rows(x, y, ref):
    ref[...] = jnp.concatenate([x, y], axis=0).T
    left = lanes_of((16, 128)) < 64
    first, second = [], []
    for i in range(4):
        p, q = (ref[pl.ds(2 * i + j, 16, stride=8), :] for j in range(2))
        first.append(jnp.where(left, p, pltpu.roll(q, 64, 1)))
        second.append(jnp.where(left, pltpu.roll(p, 64, 1), q))
    return jnp.concatenate(first, axis=1), jnp.concatenate(second, axis=1)


def to_columns(x, w, u):
    hi, lo = split(x)
    rows = x.shape[0]
    r = dot(jnp.concatenate([hi, lo], axis=0), w[u, 0])
    return r[:rows] + r[rows:] + dot(hi, w[u, 1])


def parts(r):
    return r[:8, :128] - r[8:, 128:], r[8:, :128] + r[:8, 128:]


def dot(a, b, ca=1, cb=0):
    return lax.dot_general(a, b, (((ca,), (cb,)), ((), ())), preferred_element_type=F32)


def rows_at(ref, count, at):
    if count > 1:
        at = pl.multiple_of(at, 2 if count == 2 else 8)
    return ref.at[pl.ds(at, count), :]


def spread(count, src, place, dst, here, send, recv):
    me = lax.axis_index("row")

    def step(i, carry):
        to = lax.rem(me + i, NROW)
        pltpu.make_async_remote_copy(
            src_ref=rows_at(src, count, place(to)),
            dst_ref=rows_at(dst, count, here),
            send_sem=send,
            recv_sem=recv,
            device_id={"row": to},
            device_id_type=MESH,
        ).start()
        return carry

    lax.fori_loop(1, NROW, step, 0)
    rows_at(dst, count, here)[...] = rows_at(src, count, place(me))[...]


def settle(ref, count, sem):
    rows = pl.ds(0, count)
    pltpu.make_async_copy(ref.at[rows], ref.at[rows], sem).wait()


def greet(axis, count):
    me = lax.axis_index(axis)

    def step(i, carry):
        pl.semaphore_signal(
            pltpu.get_barrier_semaphore(),
            inc=1,
            device_id={axis: me ^ (count - i)},
            device_id_type=MESH,
        )
        return carry

    lax.fori_loop(1, count, step, 0)


def await_all(count):
    pl.semaphore_wait(pltpu.get_barrier_semaphore(), count)


def rows16(ref, i):
    return ref.at[pl.ds(pl.multiple_of(16 * i, 16), 16), :]


def pass_on(src, dst, to, harm, send, recv):
    @pl.when(to != harm)
    def _():
        pltpu.make_async_remote_copy(
            src_ref=src,
            dst_ref=dst,
            send_sem=send,
            recv_sem=recv,
            device_id={"harm": to},
            device_id_type=MESH,
        ).start()

    @pl.when(to == harm)
    def _():
        dst[...] = src[...]


def trig(k, n):
    angle = 2.0 * math.pi * ((k * n) % SAMPLES) / SAMPLES
    return math.cos(angle), math.sin(angle)


def waves(volts):
    out = [None] * SAMPLES
    for n in range(9):
        sums = [None] * 4
        for h in range(HARMS):
            c, s = trig(h + 1, n)
            for i, x in (((h + 1) % 2, volts[h][0] * c), (2 + (h + 1) % 2, volts[h][1] * s)):
                sums[i] = x if sums[i] is None else sums[i] + x
        ce, co, se, so = sums
        p, m, u, v = ce + co, ce - co, se + so, se - so
        out[n] = p - u
        out[16 + n] = m - v
        if n:
            out[16 - n] = m + v
            out[SAMPLES - n] = p + u
    return out


def harmonics(x, numbers):
    sums = [[None, None] for _ in numbers]
    odd = numbers[0] % 2
    for n in range(9):
        if n in (0, 8):
            a, d = x[n], x[16 + n]
            even, flat = (a - d, a - d) if odd else (a + d, a + d)
        else:
            a, b, c, d = x[n], x[SAMPLES - n], x[16 - n], x[16 + n]
            even = (a + b) - (c + d) if odd else (a + b) + (c + d)
            flat = (a - b) + (c - d) if odd else (a - b) - (c - d)
        for i, k in enumerate(numbers):
            for part, (y, w) in enumerate(zip((even, flat), trig(k, n))):
                if abs(w) < 1e-12:
                    continue
                y = y * (w * 2.0 / SAMPLES)
                sums[i][part] = y if sums[i][part] is None else sums[i][part] + y
    return sums


def kernel(
    cur_hbm, inc_hbm, bias_hbm, pw_hbm, turn_hbm, g_hbm, w1_hbm, e2_hbm, e3_hbm, w4_hbm, out,
    cur, inc, bias, pw, turn, g, w1, e2, e3, w4, tx1, rx1, zb, yb, txv, rxv, txr, rxr, tr, vinc, vf, ff,
    level, hs, hr, ds, dr, load, send, recv,
):
    harm = lax.axis_index("harm")
    x, zhi = harm // 2, lax.rem(harm, 2)
    greet("harm", HARMS)
    greet("row", NROW)
    pairs = [(cur_hbm, cur)] + [(w1_hbm.at[j], w1.at[j]) for j in range(4)]
    pairs += [(bias_hbm, bias), (pw_hbm, pw), (turn_hbm, turn), (e2_hbm, e2), (g_hbm, g), (e3_hbm, e3)]
    pairs += [(inc_hbm, inc), (w4_hbm, w4)]
    loads = [pltpu.make_async_copy(a, b, load.at[i]) for i, (a, b) in enumerate(pairs)]
    for c in loads:
        c.start()

    loads[0].wait()
    hi, lo = split(cur[...].reshape(64, 512))
    both = jnp.concatenate([hi, lo], axis=0)
    for j in range(4):
        loads[1 + j].wait()
        r1 = dot(both, w1[j, 0])
        r = r1[:64] + r1[64:] + dot(hi, w1[j, 1])
        r = r.reshape(4, 2, 8, 512)
        for half in range(2):
            c, s = r[..., 128 * half : 128 * half + 128], r[..., 256 + 128 * half : 384 + 128 * half]
            v = [c[b, 0] + s[b, 1] for b in range(4)] + [c[b, 1] - s[b, 0] for b in range(4)]
            for i, y in enumerate(swap_blocks(v)):
                at = 8 * (16 * j + i) + 4 * half
                tx1[at : at + 4, :] = y[:4]
                tx1[at + 64 : at + 68, :] = y[4:]
    loads[5].wait()
    own = bias[...].astype(F32)
    level[0:8, :] = jnp.concatenate([own, own], axis=1)

    row = lax.axis_index("row")
    await_all(HARMS + NROW - 2)
    spread(8, tx1, lambda d: 8 * d, rx1, 8 * row, send.at[0], recv.at[0])
    swap = pltpu.make_async_remote_copy(
        src_ref=level.at[pl.ds(0, 8), :],
        dst_ref=level.at[pl.ds(8, 8), :],
        send_sem=send.at[5],
        recv_sem=recv.at[5],
        device_id={"harm": harm + 1 - 2 * zhi},
        device_id_type=MESH,
    )
    swap.start()
    for c in loads[6:]:
        c.wait()
    for p in range(2):
        vinc[p] = pw[0] * inc[0, p] + pw[1] * inc[1, p] + pw[2] * inc[2, p] + pw[3] * inc[3, p]
    tc = [turn[t : t + 1, :] for t in range(8)]
    ts = [turn[8 + t : 9 + t, :] for t in range(8)]
    left = lanes_of((64, 128)) < 64

    def rows_inverse(i):
        hi, lo = split(yb[i])
        r = dot(e3[...], jnp.concatenate([hi, lo, hi], axis=1), 1, 1)
        s = pltpu.roll(r[64:], 64, 1)
        return r[:64] + jnp.where(left, -s, s)

    settle(rx1, 504, recv.at[0])
    for half in range(2):
        for t in range(4):
            hi, lo = split(rx1[pl.ds(4 * half + t, 64, stride=8), :])
            r = dot(jnp.concatenate([hi, lo, hi], axis=0), e2[t], 0, 0)
            p, q = r[:, :128], r[:, 128:]
            zb[t, 0], zb[t, 1] = p[:32] + q[32:64], p[32:64] - q[:32]
            re, im = p[64:96] + q[96:], p[96:] - q[64:96]
            zb[4 + t, 0], zb[4 + t, 1] = re * tc[4] + im * ts[4], im * tc[4] - re * ts[4]
        for c in range(4):
            at = slice(8 * c, 8 * c + 8)
            z = dft8([(zb[t, 0, at, :], zb[t, 1, at, :]) for t in range(8)], -1)
            for q in range(8):
                zb[q, 0, at, :], zb[q, 1, at, :] = z[q]

        def keep(i, f):
            for t, (re, im) in enumerate(dft8(f, 1)):
                if t:
                    re, im = re * tc[t] - im * ts[t], im * tc[t] + re * ts[t]
                yb[4 * half + i, 8 * t : 8 * t + 8, :] = re
                yb[4 * half + i, 64 + 8 * t : 72 + 8 * t, :] = im

        port = None
        for b in range(4):
            f = []
            for q in range(8):
                re = im = None
                for c in range(4):
                    sr, si = zb[q, 0, 8 * c : 8 * c + 8, :], zb[q, 1, 8 * c : 8 * c + 8, :]
                    gr, gi = (
                        g[b, c, p, 8 * half : 8 * half + 8, 128 * q : 128 * q + 128] for p in range(2)
                    )
                    u, w = gr * sr - gi * si, gr * si + gi * sr
                    re, im = (u, w) if c == 0 else (re + u, im + w)
                f.append((re, im))
            if b < 3:
                keep(b + 1, f)
            terms = [(pw[b] * re, pw[b] * im) for re, im in f]
            port = terms if b == 0 else [(v[0] + w[0], v[1] + w[1]) for v, w in zip(port, terms)]
        keep(0, port)
        txv[pl.ds(half, 64, stride=2), :] = rows_inverse(4 * half)
    spread(2, txv, lambda d: 2 * d, rxv, 2 * row, send.at[1], recv.at[1])
    for half in range(2):
        for i in range(3):
            txr[pl.ds(3 * half + i, 64, stride=8), :] = rows_inverse(4 * half + 1 + i)
    spread(6, txr, lambda d: 8 * d, rxr, 8 * row, send.at[2], recv.at[2])

    def block(i, half):
        return rxr[pl.ds(3 * half + i, 64, stride=8), :]

    settle(rxv, 126, recv.at[1])
    x0, x1 = to_rows(*(rxv[pl.ds(half, 64, stride=2), :] for half in range(2)), tr.at[0])
    for i in range(4):
        u = lax.rem(x + 1 + i, 4)
        at = pl.ds(pl.multiple_of(128 * u, 128), 128)
        for p, y in enumerate(parts(to_columns(x0, w4.at[0], u) + to_columns(x1, w4.at[1], u))):
            vf[p, :, at] = y
            hs[pl.ds(pl.multiple_of(16 * u + 8 * p, 8), 8), :] = y + vinc[p, :, at]
        for z in range(2):
            pass_on(rows16(hs, u), rows16(hr, harm), 2 * u + lax.rem(z + 1 + zhi, 2), harm, send.at[3], recv.at[3])

    settle(rxr, 378, recv.at[2])
    both = [to_rows(block(i, 0), block(i, 1), tr.at[1 + i]) for i in range(3)]
    xa = [jnp.concatenate([both[i][half] for i in range(3)], axis=0) for half in range(2)]
    for u in range(4):
        r = to_columns(xa[0], w4.at[0], u) + to_columns(xa[1], w4.at[1], u)
        for i in range(3):
            for p, y in enumerate(parts(r[16 * i : 16 * i + 16])):
                ff[i, p, :, 128 * u : 128 * u + 128] = y
    swap.wait()
    left = lanes_of((8, 128)) < 64
    own, other = level[0:8, :], level[8:16, :]
    cap = 0.05 + 0.02 * jnp.where(left == (zhi == 0), own, other)
    settle(hr, 112, recv.at[3])

    volts = [(hr[16 * h : 16 * h + 8, :], hr[16 * h + 8 : 16 * h + 16, :]) for h in range(HARMS)]
    conduct, charge = [], []
    for w in waves(volts):
        conduct.append(0.05 * (jnp.exp(w * 0.25) - 1.0))
        charge.append(cap * (w + 0.2 * w * w))
    for z in range(2):

        @pl.when(zhi == z)
        def _():
            numbers = [2 * i + z + 1 for i in range(4)]
            for i, (k, (cc, cn), (qc, qn)) in enumerate(
                zip(numbers, harmonics(conduct, numbers), harmonics(charge, numbers))
            ):
                ds[16 * i : 16 * i + 8, :] = cc + (0.25 * k) * qn
                ds[16 * i + 8 : 16 * i + 16, :] = (0.25 * k) * qc - cn

    def hand_back(i, carry):
        to = lax.rem(x + 1 + i, 4)
        pass_on(rows16(ds, to), rows16(dr, x), 2 * to + zhi, harm, send.at[4], recv.at[4])
        return carry

    lax.fori_loop(0, 4, hand_back, 0)

    last = 1.0 / jnp.full((8, 128), pw[3], F32)
    settle(dr, 48, recv.at[4])
    for u in range(4):
        at = slice(128 * u, 128 * u + 128)
        for p in range(2):
            diode = dr[16 * u + 8 * p : 16 * u + 8 * p + 8, :]
            rest = vf[p, :, at]
            for b in range(3):
                y = ff[b, p, :, at]
                rest = rest - pw[b] * y
                out[b, p, :, at] = y + inc[b, p, :, at] - pw[b] * diode
            out[3, p, :, at] = rest * last + inc[3, p, :, at] - pw[3] * diode
    for i, (ref, count) in enumerate(
        ((tx1, 504), (txv, 126), (txr, 378), (hr, 112), (ds, 48))
    ):
        settle(ref, count, send.at[i])


def body(currents, incident, green, port_weights, bias_level):
    w1, e2, e3, w4, turn = (jnp.asarray(t) for t in tables())
    vmem = pl.BlockSpec(memory_space=pltpu.VMEM)
    anyw = pl.BlockSpec(memory_space=pltpu.HBM)
    args = (currents[0], incident[0], bias_level, port_weights, turn, green[0], w1, e2, e3, w4)
    out = pl.pallas_call(
        kernel,
        out_shape=pltpu.VMEM((4, 2, 8, 512), F32),
        in_specs=[anyw] * 10,
        out_specs=vmem,
        scratch_shapes=[
            pltpu.VMEM((4, 2, 8, 512), F32),
            pltpu.VMEM((4, 2, 8, 512), F32),
            pltpu.VMEM((8, 64), jnp.int32),
            pltpu.SMEM((4,), F32),
            pltpu.VMEM((16, 128), F32),
            pltpu.VMEM((4, 4, 2, 16, 1024), F32),
            pltpu.VMEM(w1.shape, BF16),
            pltpu.VMEM(e2.shape, BF16),
            pltpu.VMEM(e3.shape, BF16),
            pltpu.VMEM(w4.shape, BF16),
            pltpu.VMEM((512, 128), F32),
            pltpu.VMEM((512, 128), F32),
            pltpu.VMEM((8, 2, 32, 128), F32),
            pltpu.VMEM((8, 128, 128), F32),
            pltpu.VMEM((128, 128), F32),
            pltpu.VMEM((128, 128), F32),
            pltpu.VMEM((512, 128), F32),
            pltpu.VMEM((512, 128), F32),
            pltpu.VMEM((4, 128, 128), F32),
            pltpu.VMEM((2, 8, 512), F32),
            pltpu.VMEM((2, 8, 512), F32),
            pltpu.VMEM((3, 2, 8, 512), F32),
            pltpu.VMEM((16, 128), F32),
            pltpu.VMEM((64, 128), F32),
            pltpu.VMEM((128, 128), F32),
            pltpu.VMEM((64, 128), F32),
            pltpu.VMEM((64, 128), F32),
            pltpu.SemaphoreType.DMA((13,)),
            pltpu.SemaphoreType.DMA((6,)),
            pltpu.SemaphoreType.DMA((6,)),
        ],
        compiler_params=pltpu.CompilerParams(
            collective_id=0, has_side_effects=True, vmem_limit_bytes=44 * 2**20
        ),
        cost_estimate=pl.CostEstimate(flops=5 * 10**9, bytes_accessed=13 * 10**6, transcendentals=16384),
    )(*(pltpu.with_memory_space_constraint(a, pltpu.HBM) for a in args))
    return out[None]


def solution(mesh):
    placed = (
        P("harm", None, None, "row", None),
        P("harm", None, None, "row", None),
        P("harm", None, None, None, "row", None),
        P(),
        P("row", "harm"),
    )
    return jax.shard_map(
        body,
        mesh=mesh,
        in_specs=placed,
        out_specs=P("harm", None, None, "row", None),
        check_vma=False,
    )
```

```python
import functools
import math

import jax
import jax.numpy as jnp
import ml_dtypes
import numpy as np
from jax import lax
from jax.experimental import pallas as pl
from jax.experimental.pallas import tpu as pltpu
from jax.sharding import PartitionSpec as P

MESH = pl.DeviceIdType.MESH
F32 = jnp.float32
BF16 = jnp.bfloat16
HARMS = 8
SAMPLES = 32
NROW = 64
PAD = 1024


def split_np(table):
    high = table.astype(ml_dtypes.bfloat16)
    low = (table - high.astype(np.float64)).astype(ml_dtypes.bfloat16)
    return high, low


def cos_sin(product, length):
    angle = 2.0 * np.pi / length * (product % length).astype(np.float64)
    return np.cos(angle), np.sin(angle)


@functools.lru_cache(maxsize=None)
def tables():
    freq = np.arange(PAD).reshape(4, 16, 2, 8).transpose(0, 2, 1, 3).reshape(4, 2, 128)
    c, s = cos_sin(np.arange(512)[None, :, None] * freq.reshape(4, 1, 256), PAD)
    w1 = np.stack(split_np(np.concatenate([c, s], axis=2)), axis=1)
    r = 8 * np.arange(64)[None, :, None] + np.arange(4)[:, None, None]
    c, s = cos_sin(r * np.arange(128)[None, None, :], PAD)
    hi, lo = split_np(np.concatenate([c, s], axis=2))
    e2 = np.concatenate([hi, hi, lo], axis=1)
    c, s = cos_sin(8 * np.arange(64)[:, None] * np.arange(128)[None, :], PAD)
    hi, lo = split_np(np.concatenate([c, s], axis=0) / float(PAD * PAD))
    e3 = np.concatenate([hi, hi, lo], axis=1)
    freq = np.arange(PAD).reshape(64, 2, 8).transpose(1, 2, 0).reshape(2, 1, 512, 1)
    c, s = cos_sin(freq * np.arange(512).reshape(1, 4, 1, 128), PAD)
    w4 = np.stack(split_np(np.concatenate([c, s], axis=3)), axis=2)
    turn = np.concatenate(cos_sin(np.arange(8)[:, None] * np.arange(128)[None, :], PAD)).astype(np.float32)
    return w1, e2, e3, w4, turn


def dft8(z, sign):
    def add(a, b):
        return (a[0] + b[0], a[1] + b[1])

    def sub(a, b):
        return (a[0] - b[0], a[1] - b[1])

    def turn(a):
        return (-a[1], a[0]) if sign > 0 else (a[1], -a[0])

    def four(a0, a1, a2, a3):
        p, m = add(a0, a2), sub(a0, a2)
        q, d = add(a1, a3), turn(sub(a1, a3))
        return [add(p, q), add(m, d), sub(p, q), sub(m, d)]

    even = four(z[0], z[2], z[4], z[6])
    odd = four(z[1], z[3], z[5], z[7])
    h = math.sqrt(0.5)
    o1, o3 = turn(odd[1]), turn(odd[3])
    odd = [
        odd[0],
        ((odd[1][0] + o1[0]) * h, (odd[1][1] + o1[1]) * h),
        turn(odd[2]),
        ((o3[0] - odd[3][0]) * h, (o3[1] - odd[3][1]) * h),
    ]
    return [add(e, o) for e, o in zip(even, odd)] + [sub(e, o) for e, o in zip(even, odd)]


def split(x):
    high = x.astype(BF16)
    return high, (x - high.astype(F32)).astype(BF16)


def lanes_of(shape):
    return lax.broadcasted_iota(jnp.int32, shape, 1)


def swap_blocks(v):
    lane = lanes_of((8, 128))
    stay = (lax.broadcasted_iota(jnp.int32, (8, 128), 0) < 4) == (lane < 64)
    v = [jnp.where(stay, x, pltpu.roll(pltpu.roll(x, 4, 0), 64, 1)) for x in v]
    for bit in (4, 2, 1):
        shift = 8 * bit
        keep = (lane & shift) == 0
        for a in range(8):
            if a & bit:
                continue
            x, y = v[a], v[a + bit]
            v[a] = jnp.where(keep, x, pltpu.roll(y, shift, 1))
            v[a + bit] = jnp.where(keep, pltpu.roll(x, 128 - shift, 1), y)
    return v


def to_rows(x, y, ref):
    ref[...] = jnp.concatenate([x, y], axis=0).T
    left = lanes_of((16, 128)) < 64
    first, second = [], []
    for i in range(4):
        p, q = (ref[pl.ds(2 * i + j, 16, stride=8), :] for j in range(2))
        first.append(jnp.where(left, p, pltpu.roll(q, 64, 1)))
        second.append(jnp.where(left, pltpu.roll(p, 64, 1), q))
    return jnp.concatenate(first, axis=1), jnp.concatenate(second, axis=1)


def to_columns(x, w, u):
    hi, lo = split(x)
    rows = x.shape[0]
    r = dot(jnp.concatenate([hi, lo], axis=0), w[u, 0])
    return r[:rows] + r[rows:] + dot(hi, w[u, 1])


def parts(r):
    return r[:8, :128] - r[8:, 128:], r[8:, :128] + r[:8, 128:]


def dot(a, b, ca=1, cb=0):
    return lax.dot_general(a, b, (((ca,), (cb,)), ((), ())), preferred_element_type=F32)


def rows_at(ref, count, at):
    if count > 1:
        at = pl.multiple_of(at, 2 if count == 2 else 8)
    return ref.at[pl.ds(at, count), :]


def spread(count, src, place, dst, here, send, recv):
    me = lax.axis_index("row")

    def step(i, carry):
        to = lax.rem(me + i, NROW)
        pltpu.make_async_remote_copy(
            src_ref=rows_at(src, count, place(to)),
            dst_ref=rows_at(dst, count, here),
            send_sem=send,
            recv_sem=recv,
            device_id={"row": to},
            device_id_type=MESH,
        ).start()
        return carry

    lax.fori_loop(1, NROW, step, 0)
    rows_at(dst, count, here)[...] = rows_at(src, count, place(me))[...]


def settle(ref, count, sem):
    rows = pl.ds(0, count)
    pltpu.make_async_copy(ref.at[rows], ref.at[rows], sem).wait()


def greet(axis, count):
    me = lax.axis_index(axis)

    def step(i, carry):
        pl.semaphore_signal(
            pltpu.get_barrier_semaphore(),
            inc=1,
            device_id={axis: me ^ (count - i)},
            device_id_type=MESH,
        )
        return carry

    lax.fori_loop(1, count, step, 0)


def await_all(count):
    pl.semaphore_wait(pltpu.get_barrier_semaphore(), count)


def rows16(ref, i):
    return ref.at[pl.ds(pl.multiple_of(16 * i, 16), 16), :]


def pass_on(src, dst, to, harm, send, recv):
    @pl.when(to != harm)
    def _():
        pltpu.make_async_remote_copy(
            src_ref=src,
            dst_ref=dst,
            send_sem=send,
            recv_sem=recv,
            device_id={"harm": to},
            device_id_type=MESH,
        ).start()

    @pl.when(to == harm)
    def _():
        dst[...] = src[...]


def trig(k, n):
    angle = 2.0 * math.pi * ((k * n) % SAMPLES) / SAMPLES
    return math.cos(angle), math.sin(angle)


def waves(volts):
    out = [None] * SAMPLES
    for n in range(9):
        sums = [None] * 4
        for h in range(HARMS):
            c, s = trig(h + 1, n)
            for i, x in (((h + 1) % 2, volts[h][0] * c), (2 + (h + 1) % 2, volts[h][1] * s)):
                sums[i] = x if sums[i] is None else sums[i] + x
        ce, co, se, so = sums
        p, m, u, v = ce + co, ce - co, se + so, se - so
        out[n] = p - u
        out[16 + n] = m - v
        if n:
            out[16 - n] = m + v
            out[SAMPLES - n] = p + u
    return out


def harmonics(x, numbers):
    sums = [[None, None] for _ in numbers]
    odd = numbers[0] % 2
    for n in range(9):
        if n in (0, 8):
            a, d = x[n], x[16 + n]
            even, flat = (a - d, a - d) if odd else (a + d, a + d)
        else:
            a, b, c, d = x[n], x[SAMPLES - n], x[16 - n], x[16 + n]
            even = (a + b) - (c + d) if odd else (a + b) + (c + d)
            flat = (a - b) + (c - d) if odd else (a - b) - (c - d)
        for i, k in enumerate(numbers):
            for part, (y, w) in enumerate(zip((even, flat), trig(k, n))):
                if abs(w) < 1e-12:
                    continue
                y = y * (w * 2.0 / SAMPLES)
                sums[i][part] = y if sums[i][part] is None else sums[i][part] + y
    return sums


def kernel(
    cur_hbm, inc_hbm, bias_hbm, pw_hbm, turn_hbm, g_hbm, w1_hbm, e2_hbm, e3_hbm, w4_hbm, out,
    cur, inc, bias, pw, turn, g, w1, e2, e3, w4, tx1, rx1, zb, yb, txv, rxv, txr, rxr, tr, vinc, vf, ff,
    level, hs, hr, ds, dr, load, send, recv,
):
    harm = lax.axis_index("harm")
    x, zhi = harm // 2, lax.rem(harm, 2)
    greet("harm", HARMS)
    greet("row", NROW)
    pairs = [(cur_hbm, cur)] + [(w1_hbm.at[j], w1.at[j]) for j in range(4)]
    pairs += [(bias_hbm, bias), (pw_hbm, pw), (turn_hbm, turn), (e2_hbm, e2), (g_hbm, g), (e3_hbm, e3)]
    pairs += [(inc_hbm, inc), (w4_hbm, w4)]
    loads = [pltpu.make_async_copy(a, b, load.at[i]) for i, (a, b) in enumerate(pairs)]
    for c in loads:
        c.start()

    loads[0].wait()
    hi, lo = split(cur[...].reshape(64, 512))
    both = jnp.concatenate([hi, lo], axis=0)
    for j in range(4):
        loads[1 + j].wait()
        r1 = dot(both, w1[j, 0])
        r = r1[:64] + r1[64:] + dot(hi, w1[j, 1])
        r = r.reshape(4, 2, 8, 512)
        for half in range(2):
            c, s = r[..., 128 * half : 128 * half + 128], r[..., 256 + 128 * half : 384 + 128 * half]
            v = [c[b, 0] + s[b, 1] for b in range(4)] + [c[b, 1] - s[b, 0] for b in range(4)]
            for i, y in enumerate(swap_blocks(v)):
                at = 8 * (16 * j + i) + 4 * half
                tx1[at : at + 4, :] = y[:4]
                tx1[at + 64 : at + 68, :] = y[4:]
    loads[5].wait()
    own = bias[...].astype(F32)
    level[0:8, :] = jnp.concatenate([own, own], axis=1)

    row = lax.axis_index("row")
    await_all(HARMS + NROW - 2)
    spread(8, tx1, lambda d: 8 * d, rx1, 8 * row, send.at[0], recv.at[0])
    swap = pltpu.make_async_remote_copy(
        src_ref=level.at[pl.ds(0, 8), :],
        dst_ref=level.at[pl.ds(8, 8), :],
        send_sem=send.at[5],
        recv_sem=recv.at[5],
        device_id={"harm": harm + 1 - 2 * zhi},
        device_id_type=MESH,
    )
    swap.start()
    for c in loads[6:]:
        c.wait()
    for p in range(2):
        vinc[p] = pw[0] * inc[0, p] + pw[1] * inc[1, p] + pw[2] * inc[2, p] + pw[3] * inc[3, p]
    tc = [turn[t : t + 1, :] for t in range(8)]
    ts = [turn[8 + t : 9 + t, :] for t in range(8)]
    left = lanes_of((64, 128)) < 64

    def rows_inverse(i):
        hi, lo = split(yb[i])
        r = dot(e3[...], jnp.concatenate([hi, lo, hi], axis=1), 1, 1)
        s = pltpu.roll(r[64:], 64, 1)
        return r[:64] + jnp.where(left, -s, s)

    settle(rx1, 504, recv.at[0])
    later = []
    for half in range(2):
        for t in range(4):
            hi, lo = split(rx1[pl.ds(4 * half + t, 64, stride=8), :])
            r = dot(jnp.concatenate([hi, lo, hi], axis=0), e2[t], 0, 0)
            p, q = r[:, :128], r[:, 128:]
            zb[t, 0], zb[t, 1] = p[:32] + q[32:64], p[32:64] - q[:32]
            re, im = p[64:96] + q[96:], p[96:] - q[64:96]
            zb[4 + t, 0], zb[4 + t, 1] = re * tc[4] + im * ts[4], im * tc[4] - re * ts[4]
        for c in range(4):
            at = slice(8 * c, 8 * c + 8)
            z = dft8([(zb[t, 0, at, :], zb[t, 1, at, :]) for t in range(8)], -1)
            for q in range(8):
                zb[q, 0, at, :], zb[q, 1, at, :] = z[q]

        def keep(i, f, half=half):
            for t, (re, im) in enumerate(dft8(f, 1)):
                if t:
                    re, im = re * tc[t] - im * ts[t], im * tc[t] + re * ts[t]
                yb[4 * half + i, 8 * t : 8 * t + 8, :] = re
                yb[4 * half + i, 64 + 8 * t : 72 + 8 * t, :] = im

        port = None
        for b in range(4):
            f = []
            for q in range(8):
                re = im = None
                for c in range(4):
                    sr, si = zb[q, 0, 8 * c : 8 * c + 8, :], zb[q, 1, 8 * c : 8 * c + 8, :]
                    gr, gi = (
                        g[b, c, p, 8 * half : 8 * half + 8, 128 * q : 128 * q + 128] for p in range(2)
                    )
                    u, w = gr * sr - gi * si, gr * si + gi * sr
                    re, im = (u, w) if c == 0 else (re + u, im + w)
                f.append((re, im))
            if b < 3:
                later.append((keep, b + 1, f))
            terms = [(pw[b] * re, pw[b] * im) for re, im in f]
            port = terms if b == 0 else [(v[0] + w[0], v[1] + w[1]) for v, w in zip(port, terms)]
        keep(0, port)
        txv[pl.ds(half, 64, stride=2), :] = rows_inverse(4 * half)
    spread(2, txv, lambda d: 2 * d, rxv, 2 * row, send.at[1], recv.at[1])
    for keep, i, f in later:
        keep(i, f)
    for half in range(2):
        for i in range(3):
            txr[pl.ds(3 * half + i, 64, stride=8), :] = rows_inverse(4 * half + 1 + i)
    spread(6, txr, lambda d: 8 * d, rxr, 8 * row, send.at[2], recv.at[2])

    def block(i, half):
        return rxr[pl.ds(3 * half + i, 64, stride=8), :]

    settle(rxv, 126, recv.at[1])
    x0, x1 = to_rows(*(rxv[pl.ds(half, 64, stride=2), :] for half in range(2)), tr.at[0])
    for i in range(4):
        u = lax.rem(x + 1 + i, 4)
        at = pl.ds(pl.multiple_of(128 * u, 128), 128)
        for p, y in enumerate(parts(to_columns(x0, w4.at[0], u) + to_columns(x1, w4.at[1], u))):
            vf[p, :, at] = y
            hs[pl.ds(pl.multiple_of(16 * u + 8 * p, 8), 8), :] = y + vinc[p, :, at]
        for z in range(2):
            pass_on(rows16(hs, u), rows16(hr, harm), 2 * u + lax.rem(z + 1 + zhi, 2), harm, send.at[3], recv.at[3])

    settle(rxr, 378, recv.at[2])
    both = [to_rows(block(i, 0), block(i, 1), tr.at[1 + i]) for i in range(3)]
    xa = [jnp.concatenate([both[i][half] for i in range(3)], axis=0) for half in range(2)]
    for u in range(4):
        r = to_columns(xa[0], w4.at[0], u) + to_columns(xa[1], w4.at[1], u)
        for i in range(3):
            for p, y in enumerate(parts(r[16 * i : 16 * i + 16])):
                ff[i, p, :, 128 * u : 128 * u + 128] = y
    swap.wait()
    left = lanes_of((8, 128)) < 64
    own, other = level[0:8, :], level[8:16, :]
    cap = 0.05 + 0.02 * jnp.where(left == (zhi == 0), own, other)
    settle(hr, 112, recv.at[3])

    volts = [(hr[16 * h : 16 * h + 8, :], hr[16 * h + 8 : 16 * h + 16, :]) for h in range(HARMS)]
    conduct, charge = [], []
    for w in waves(volts):
        conduct.append(0.05 * (jnp.exp(w * 0.25) - 1.0))
        charge.append(cap * (w + 0.2 * w * w))
    for z in range(2):

        @pl.when(zhi == z)
        def _():
            numbers = [2 * i + z + 1 for i in range(4)]
            for i, (k, (cc, cn), (qc, qn)) in enumerate(
                zip(numbers, harmonics(conduct, numbers), harmonics(charge, numbers))
            ):
                ds[16 * i : 16 * i + 8, :] = cc + (0.25 * k) * qn
                ds[16 * i + 8 : 16 * i + 16, :] = (0.25 * k) * qc - cn

    def hand_back(i, carry):
        to = lax.rem(x + 1 + i, 4)
        pass_on(rows16(ds, to), rows16(dr, x), 2 * to + zhi, harm, send.at[4], recv.at[4])
        return carry

    lax.fori_loop(0, 4, hand_back, 0)

    last = 1.0 / jnp.full((8, 128), pw[3], F32)
    for u in range(4):
        at = slice(128 * u, 128 * u + 128)
        for p in range(2):
            rest = vf[p, :, at]
            for b in range(3):
                y = ff[b, p, :, at]
                rest = rest - pw[b] * y
                out[b, p, :, at] = y + inc[b, p, :, at]
            out[3, p, :, at] = rest * last + inc[3, p, :, at]
    settle(dr, 48, recv.at[4])
    for u in range(4):
        at = slice(128 * u, 128 * u + 128)
        for p in range(2):
            diode = dr[16 * u + 8 * p : 16 * u + 8 * p + 8, :]
            for b in range(4):
                out[b, p, :, at] = out[b, p, :, at] - pw[b] * diode
    for i, (ref, count) in enumerate(
        ((tx1, 504), (txv, 126), (txr, 378), (hr, 112), (ds, 48))
    ):
        settle(ref, count, send.at[i])


def body(currents, incident, green, port_weights, bias_level):
    w1, e2, e3, w4, turn = (jnp.asarray(t) for t in tables())
    vmem = pl.BlockSpec(memory_space=pltpu.VMEM)
    anyw = pl.BlockSpec(memory_space=pltpu.HBM)
    args = (currents[0], incident[0], bias_level, port_weights, turn, green[0], w1, e2, e3, w4)
    out = pl.pallas_call(
        kernel,
        out_shape=pltpu.VMEM((4, 2, 8, 512), F32),
        in_specs=[anyw] * 10,
        out_specs=vmem,
        scratch_shapes=[
            pltpu.VMEM((4, 2, 8, 512), F32),
            pltpu.VMEM((4, 2, 8, 512), F32),
            pltpu.VMEM((8, 64), jnp.int32),
            pltpu.SMEM((4,), F32),
            pltpu.VMEM((16, 128), F32),
            pltpu.VMEM((4, 4, 2, 16, 1024), F32),
            pltpu.VMEM(w1.shape, BF16),
            pltpu.VMEM(e2.shape, BF16),
            pltpu.VMEM(e3.shape, BF16),
            pltpu.VMEM(w4.shape, BF16),
            pltpu.VMEM((512, 128), F32),
            pltpu.VMEM((512, 128), F32),
            pltpu.VMEM((8, 2, 32, 128), F32),
            pltpu.VMEM((8, 128, 128), F32),
            pltpu.VMEM((128, 128), F32),
            pltpu.VMEM((128, 128), F32),
            pltpu.VMEM((512, 128), F32),
            pltpu.VMEM((512, 128), F32),
            pltpu.VMEM((4, 128, 128), F32),
            pltpu.VMEM((2, 8, 512), F32),
            pltpu.VMEM((2, 8, 512), F32),
            pltpu.VMEM((3, 2, 8, 512), F32),
            pltpu.VMEM((16, 128), F32),
            pltpu.VMEM((64, 128), F32),
            pltpu.VMEM((128, 128), F32),
            pltpu.VMEM((64, 128), F32),
            pltpu.VMEM((64, 128), F32),
            pltpu.SemaphoreType.DMA((13,)),
            pltpu.SemaphoreType.DMA((6,)),
            pltpu.SemaphoreType.DMA((6,)),
        ],
        compiler_params=pltpu.CompilerParams(
            collective_id=0, has_side_effects=True, vmem_limit_bytes=44 * 2**20
        ),
        cost_estimate=pl.CostEstimate(flops=5 * 10**9, bytes_accessed=13 * 10**6, transcendentals=16384),
    )(*(pltpu.with_memory_space_constraint(a, pltpu.HBM) for a in args))
    return out[None]


def solution(mesh):
    placed = (
        P("harm", None, None, "row", None),
        P("harm", None, None, "row", None),
        P("harm", None, None, None, "row", None),
        P(),
        P("row", "harm"),
    )
    return jax.shard_map(
        body,
        mesh=mesh,
        in_specs=placed,
        out_specs=P("harm", None, None, "row", None),
        check_vma=False,
    )
```
